32 devices in a mesh: group: 8 (over y, x, core), expert: 4 (over z).
Axes of the slice: x: 2, y: 2, z: 4, core: 2. Of those that a mesh axis runs over, the one named last changes fastest.
Arguments:
- tokens: bfloat16 [4096, 1536], P(('group', 'expert')), may hold values from -6 to 6
- gate_train: float32 [8, 1536, 512], P('expert', 'group'), may hold values from -0.15625 to 0.15625
- up_train: float32 [8, 1536, 512], P('expert', 'group'), may hold values from -0.15625 to 0.15625
- down_train: float32 [8, 512, 1536], P('expert', None, 'group'), may hold values from -0.25 to 0.25
- routes: int32 [4096, 6], P(('group', 'expert')), may hold values from 0 to 7, as said below
- route_scores: float32 [4096, 6], P(('group', 'expert')), may hold values from 0.05 to 1
- live: int32 [4096], P(('group', 'expert')), may hold values from 0 to 1
Outputs:
- moe_out: bfloat16 [4096, 1536], P(('group', 'expert'))
The draws below stay inside these ranges and needn't reach their ends.
Inputs may be any that keep to these rules, and one draw needn't show every extreme that they name: `routes`: each row names 6 different experts; one expert, the same on every device, is named by at least 96 live rows among each device's 128 rows.
All inputs are finite; a program needn't handle non-finite values.
Results may differ from the reference program's by a relative error of at most 0.0075.
Values may be sent and summed in bfloat16 or wider, within the bound.
A program may use at most 64 MiB of HBM per device.

```python
import math
import jax
import jax.numpy as jnp
from jax import lax

D = 1536
FF = 512
TOP = 6
TOK_DEV = 128
EXPERT_TOTAL = 8
CAP = 96
TOKEN_TOTAL = 4096


def route_helper(key):
    blocks = TOKEN_TOTAL // TOK_DEV
    forced_count = min(TOK_DEV - 2, CAP + CAP // 2 + 1)
    ordering_key, popular_key, boost_key, scoring_key, active_key = jax.random.split(key, 5)
    order_keys = jax.random.randint(ordering_key, (blocks, TOK_DEV), 0, 1 << 20, dtype=jnp.int32) * TOK_DEV + jnp.arange(TOK_DEV, dtype=jnp.int32)[None, :]
    order_rank = jnp.argsort(jnp.argsort(order_keys, axis=1), axis=1)
    forced = (order_rank < forced_count).reshape(TOKEN_TOTAL)
    hot_expert = jax.random.randint(popular_key, (), 0, EXPERT_TOTAL, dtype=jnp.int32)
    expert_ids = jnp.arange(EXPERT_TOTAL, dtype=jnp.int32)
    score_boost = jax.random.randint(boost_key, (EXPERT_TOTAL,), 0, 3, dtype=jnp.int32) * (1 << 18)
    router_scores = jax.random.randint(scoring_key, (TOKEN_TOTAL, EXPERT_TOTAL), 0, 1 << 20, dtype=jnp.int32) + score_boost[None, :]
    router_scores = router_scores + jnp.where(forced[:, None] & (expert_ids[None, :] == hot_expert), 1 << 23, 0).astype(jnp.int32)
    router_scores = router_scores * EXPERT_TOTAL + expert_ids[None, :]
    values, chosen = lax.top_k(router_scores, TOP)
    random_live = jax.random.randint(active_key, (TOKEN_TOTAL,), 0, 4, dtype=jnp.int32) > 0
    live_rows = jnp.where(forced | random_live, 1, 0).astype(jnp.int32)
    return (chosen.astype(jnp.int32), live_rows)


def draw_routes(key, part):
    return route_helper(jax.random.fold_in(key, 4242))[0]


def draw_live(key, part):
    return route_helper(jax.random.fold_in(key, 4242))[1]


def shard_levels(stream_key, extent, cuts, least, high):
    loudness = 1.0
    for dim, blocks in cuts:
        draws = jax.random.uniform(jax.random.fold_in(jax.random.fold_in(stream_key, 6), dim), (blocks,), jnp.float32, least / len(cuts), high / len(cuts))
        loudness = loudness * jnp.repeat(jnp.exp(draws), extent[dim] // blocks).reshape((-1,) + (1,) * (len(extent) - 1 - dim))
    return loudness


def bell_draw(key, shape, spread, bound, pieces=(), kind=jnp.bfloat16):
    result = jax.random.normal(key, shape, jnp.float32) * spread
    if len(pieces) > 0:
        result = shard_levels(key, shape, pieces, -0.22, 0.18) * result
    return jnp.clip(result, min=-bound, max=bound).astype(kind)


def setup_inputs(seed: int = 0) -> dict:
    keys = jax.random.split(jax.random.key(seed), 8)
    tokens = bell_draw(keys[0], (TOKEN_TOTAL, D), 1.0, 6.0, ((0, 32),))
    gate_train = bell_draw(keys[1], (EXPERT_TOTAL, D, FF), D ** -0.5, 0.15625, ((0, 4), (1, 8)), jnp.float32)
    up_train = bell_draw(keys[2], (EXPERT_TOTAL, D, FF), D ** -0.5, 0.15625, ((0, 4), (1, 8)), jnp.float32)
    down_train = bell_draw(keys[3], (EXPERT_TOTAL, FF, D), FF ** -0.5, 0.25, ((0, 4), (2, 8)), jnp.float32)
    routes = draw_routes(jax.random.fold_in(keys[7], 71), 0)
    route_scores = jnp.clip(jnp.exp(math.log(1.0) - 2.9957323 * jax.random.uniform(keys[5], (TOKEN_TOTAL, TOP), jnp.float32) ** shard_levels(keys[5], (TOKEN_TOTAL, TOP), ((0, 32),), -0.2, 0.2)), 0.05, 1.0)
    live = draw_live(jax.random.fold_in(keys[7], 71), 0)
    return {"tokens": tokens, "gate_train": gate_train, "up_train": up_train, "down_train": down_train, "routes": routes, "route_scores": route_scores, "live": live}


def reference(tokens, gate_train, up_train, down_train, routes, route_scores, live):
    gate_up_w = jnp.concatenate([gate_train, up_train], axis=2).astype(jnp.bfloat16)
    down_w = down_train.astype(jnp.bfloat16)
    blocks = TOKEN_TOTAL // TOK_DEV
    route_share = route_scores / jnp.sum(route_scores, axis=1, keepdims=True)
    route_flat = routes.reshape(blocks, TOK_DEV * TOP)
    live_flat = jnp.repeat(live.reshape(blocks, TOK_DEV), TOP, axis=1)
    expert_ids = jnp.arange(EXPERT_TOTAL, dtype=jnp.int32)
    onehot = ((route_flat[:, :, None] == expert_ids[None, None, :]) & (live_flat[:, :, None] > 0)).astype(jnp.int32)
    earlier = jnp.cumsum(onehot, axis=1) - onehot
    slot_index = jnp.sum(earlier * onehot, axis=2)
    kept_mask = (live_flat > 0) & (slot_index < CAP)
    block_ids = jnp.arange(blocks, dtype=jnp.int32)[:, None]
    request_ids = jnp.arange(TOK_DEV * TOP, dtype=jnp.int32)[None, :]
    token_row = (block_ids * TOK_DEV + request_ids // TOP).astype(jnp.int32)
    total_slots = EXPERT_TOTAL * blocks * CAP
    position = jnp.where(kept_mask, route_flat * (blocks * CAP) + block_ids * CAP + slot_index, total_slots).astype(jnp.int32)
    position = position.reshape(-1)
    table_row = jnp.zeros((total_slots,), jnp.int32).at[position].set(token_row.reshape(-1).astype(jnp.int32), mode="drop")
    table_share = jnp.zeros((total_slots,), route_share.dtype).at[position].set(route_share.reshape(-1), mode="drop")
    table_row = table_row.reshape(EXPERT_TOTAL, blocks * CAP)
    table_share = table_share.reshape(EXPERT_TOTAL, blocks * CAP)

    def one_expert(running, inputs):
        weight_gu, weight_down, rows_here, shares_here = inputs
        picked = tokens[rows_here]
        gate_up = jnp.dot(picked, weight_gu, preferred_element_type=jnp.float32)
        hidden = (jax.nn.silu(gate_up[:, :FF]) * gate_up[:, FF:]).astype(jnp.bfloat16)
        expert_rows = jnp.dot(hidden, weight_down, preferred_element_type=jnp.float32).astype(jnp.bfloat16)
        running = running.at[rows_here].add(shares_here[:, None].astype(jnp.float32) * expert_rows.astype(jnp.float32))
        return running, None

    start_acc = jnp.zeros((TOKEN_TOTAL, D), jnp.float32)
    summed, nothing = lax.scan(one_expert, start_acc, (gate_up_w, down_w, table_row, table_share))
    return summed.astype(jnp.bfloat16)
```

```python
import functools

import jax
import jax.numpy as jnp
from jax import lax
from jax.experimental import pallas as pl
from jax.experimental.pallas import tpu as pltpu
from jax.sharding import PartitionSpec as P

MESH = pl.DeviceIdType.MESH
F32, BF16 = jnp.float32, jnp.bfloat16
PAIR = (((1,), (1,)), ((), ()))


def xor(value, mask):
    bit = 1
    while bit <= mask:
        if mask & bit:
            value = value + bit * (1 - 2 * ((value // bit) % 2))
        bit *= 2
    return value


def kernel(
    n_group, n_hold, capacity,
    tokens, gate, up, down, routes, scores, live, out,
    w_gu, w_down, tok_all, share_out, share_in, hidden, stage, back, flip, down_flip,
    gu_send, gu_recv, down_send, down_recv, tok_send, tok_recv, share_send, share_recv,
    ret_send, ret_recv,
):
    local, rows, ff = gate.shape
    block, width = tokens.shape
    top = routes.shape[1]
    experts = local * n_hold
    chips = n_group // 2
    square = chips == 4
    me, holder = lax.axis_index("group"), lax.axis_index("expert")
    chip = me // 2
    sibling = xor(me, 1)

    def device(group, expert):
        return (group, expert)

    def peer(d):
        return lax.rem(holder + d, n_hold)

    def origin(d):
        return lax.rem(holder + n_hold - d, n_hold)

    near = (1, 2) if square else tuple(range(1, chips))
    barrier = pltpu.get_barrier_semaphore()
    partners = [device(xor(me, 2 * j), holder) for j in near] + [device(sibling, holder)]
    partners += [device(me, peer(d)) for d in range(1, n_hold)]
    for partner in partners:
        pl.semaphore_signal(barrier, inc=1, device_id=partner, device_id_type=MESH)

    mine = pl.multiple_of(me * rows, rows)
    for e in range(local):
        w_gu[e, pl.ds(mine, rows), :ff] = gate[e].astype(BF16)
        w_gu[e, pl.ds(mine, rows), ff:] = up[e].astype(BF16)
    pl.semaphore_wait(barrier, len(partners))

    started = []

    def start(src, dst, send, recv, target):
        copy = pltpu.make_async_remote_copy(
            src_ref=src, dst_ref=dst, send_sem=send, recv_sem=recv,
            device_id=target, device_id_type=MESH,
        )
        copy.start()
        started.append(copy)

    halves = 2 if square else 1
    half_rows = rows // halves

    def piece(kind, key, owner):
        base = pl.multiple_of(owner * rows + key[-1] * half_rows, half_rows)
        if kind == "gu":
            return w_gu.at[key[0], pl.ds(base, half_rows), :]
        return w_down.at[pl.ds(base, half_rows), :]

    def sems(kind, key):
        if kind == "gu":
            index = key[0] * halves + key[1]
            return gu_send, gu_recv, index
        return down_send, down_recv, key[0]

    def send_piece(kind, key, owner, slot, target):
        send, recv, index = sems(kind, key)
        ref = piece(kind, key, owner)
        start(ref, ref, send.at[index, slot], recv.at[index, slot], device(target, holder))

    def wait_piece(kind, key, owner, slot):
        send, recv, index = sems(kind, key)
        ref = piece(kind, key, owner)
        pltpu.make_async_remote_copy(
            src_ref=ref, dst_ref=ref, send_sem=send.at[index, slot], recv_sem=recv.at[index, slot],
            device_id=device(sibling, holder), device_id_type=MESH,
        ).wait_recv()

    def send_own(kind, keys):
        for key in keys:
            order = near if key[-1] == 0 else near[::-1]
            for j in order:
                send_piece(kind, key, me, j, xor(me, 2 * j))
        for key in keys:
            send_piece(kind, key, me, chips, sibling)

    def service_near(kind, keys):
        for key in keys:
            for j in near:
                owner = xor(me, 2 * j)
                wait_piece(kind, key, owner, j)
                if square and (j == 1) == (key[-1] == 0):
                    send_piece(kind, key, owner, 3, xor(me, 2 * (3 - j)))
                send_piece(kind, key, owner, chips + j, sibling)

    def service_far(kind, keys):
        if square:
            for key in keys:
                owner = xor(me, 6)
                wait_piece(kind, key, owner, 3)
                send_piece(kind, key, owner, chips + 3, sibling)

    def wait_sibling(kind, keys, j):
        for key in keys:
            wait_piece(kind, key, xor(sibling, 2 * j), chips + j)

    gu_keys = [[(e, a) for a in range(halves)] for e in range(local)]
    down_keys = [(a,) for a in range(halves)]

    send_own("gu", gu_keys[0])
    for d in range(1, n_hold):
        start(tokens, tok_all.at[d], tok_send.at[d], tok_recv.at[d], device(me, peer(d)))
    for e in range(1, local):
        send_own("gu", gu_keys[e])

    flip[...] = jnp.zeros_like(flip)
    flip[:, :top] = routes[...].astype(F32)
    flip[:, 8:8 + top] = scores[...]
    turned = flip[...].T
    named_expert = turned[:top]
    chosen = turned[8:8 + top]
    chosen = chosen / jnp.sum(chosen, axis=0, keepdims=True)
    expert_id = lax.broadcasted_iota(jnp.int32, (experts, block), 0).astype(F32)
    weight = jnp.zeros((experts, block), F32)
    named = jnp.zeros((experts, block), F32)
    for k in range(top):
        hit = named_expert[k:k + 1] == expert_id
        weight = weight + jnp.where(hit, chosen[k:k + 1], 0.0)
        named = named + jnp.where(hit, 1.0, 0.0)
    alive = (live[...] > 0).astype(F32)
    named = named * alive
    before = (
        lax.broadcasted_iota(jnp.int32, (block, block), 0)
        < lax.broadcasted_iota(jnp.int32, (block, block), 1)
    ).astype(BF16)
    earlier = jnp.dot(named.astype(BF16), before, preferred_element_type=F32)
    weight = jnp.where((earlier < capacity) & (alive > 0), weight, 0.0)
    share_out[...] = jnp.zeros_like(share_out)
    for p in range(n_hold):
        share_out[p, :local, :] = weight[p * local:(p + 1) * local]
    for d in range(1, n_hold):
        start(
            share_out.at[peer(d)], share_in.at[d], share_send.at[d], share_recv.at[d],
            device(me, peer(d)),
        )

    for e in range(local):
        down_flip[:, :rows] = down[e]
        w_down[pl.ds(mine, rows), e * ff:(e + 1) * ff] = (
            down_flip[...].T[:rows].astype(BF16)
        )
    tok_all[0] = tokens[...]
    share_in[0] = share_out[holder]

    for e in range(local):
        service_near("gu", gu_keys[e])
        if e > 0:
            service_far("gu", gu_keys[e - 1])
    send_own("down", down_keys)
    service_far("gu", gu_keys[local - 1])
    for e in range(local):
        for j in range(chips):
            wait_sibling("gu", gu_keys[e], j)

    tile = 256
    per_group = 2

    def wait_tokens(d):
        for src, dst, send, recv in (
            (tokens, tok_all.at[d], tok_send.at[d], tok_recv.at[d]),
            (share_out.at[0], share_in.at[d], share_send.at[d], share_recv.at[d]),
        ):
            pltpu.make_async_remote_copy(
                src_ref=src, dst_ref=dst, send_sem=send, recv_sem=recv,
                device_id=device(sibling, holder), device_id_type=MESH,
            ).wait_recv()

    def hidden_group(first):
        count = per_group * block
        flip[: per_group * 8] = share_in[first:first + per_group].reshape(per_group * 8, block)
        columns = flip[...].T
        picked = tok_all[first:first + per_group].reshape(count, width)
        for e in range(local):
            scale = jnp.concatenate(
                [columns[:, i * 8 + e:i * 8 + e + 1] for i in range(per_group)], axis=0
            )

            def body(j, carry):
                at = pl.multiple_of(j * tile, tile)
                g = jnp.dot(picked, w_gu[e, :, pl.ds(at, tile)], preferred_element_type=F32)
                u = jnp.dot(
                    picked, w_gu[e, :, pl.ds(pl.multiple_of(ff + at, tile), tile)],
                    preferred_element_type=F32,
                )
                value = (g / (1.0 + jnp.exp(-g))) * u * scale
                hidden[first * block:first * block + count,
                       pl.ds(pl.multiple_of(e * ff + at, tile), tile)] = value.astype(BF16)
                return carry

            lax.fori_loop(0, ff // tile, body, 0)

    for first in range(0, n_hold, per_group):
        if first == per_group or n_hold == per_group:
            service_near("down", down_keys)
        for d in range(first, first + per_group):
            if d > 0:
                wait_tokens(d)
        hidden_group(first)

    parts, piece_width = back.shape[1], back.shape[3]

    def column(part):
        if parts == 1:
            return 0
        return pl.multiple_of(xor(chip, part) * piece_width, piece_width)

    for part in range(parts):
        if parts == 1:
            service_far("down", down_keys)
            for j in range(chips):
                wait_sibling("down", down_keys, j)
        else:
            if part == min(2, parts - 1):
                service_far("down", down_keys)
            wait_sibling("down", down_keys, part)
        at = column(part)
        for first in range(0, n_hold, 4):
            count = min(4, n_hold - first)
            value = lax.dot_general(
                hidden[first * block:(first + count) * block, :],
                w_down[pl.ds(at, piece_width), :], PAIR, preferred_element_type=F32,
            )
            stage[first:first + count, part] = value.astype(BF16).reshape(
                count, block, piece_width
            )
        for d in range(n_hold - 1, 0, -1):
            start(
                stage.at[d, part], back.at[d, part], ret_send.at[d, part], ret_recv.at[d, part],
                device(me, origin(d)),
            )

    for part in range(parts):
        total = stage[0, part].astype(F32)
        for d in range(1, n_hold):
            pltpu.make_async_remote_copy(
                src_ref=stage.at[d, part], dst_ref=back.at[d, part],
                send_sem=ret_send.at[d, part], recv_sem=ret_recv.at[d, part],
                device_id=device(sibling, holder), device_id_type=MESH,
            ).wait_recv()
            total = total + back[d, part].astype(F32)
        out[:, pl.ds(column(part), piece_width)] = total.astype(BF16)

    for copy in started:
        copy.wait_send()


def local(n_group, n_hold, tokens, gate, up, down, routes, scores, live):
    experts_here, rows, ff = gate.shape
    block, width = tokens.shape
    top = routes.shape[1]
    capacity = block * top // (experts_here * n_hold)
    chips = n_group // 2
    halves = 2 if chips == 4 else 1
    parts = chips if (2 * rows) % 128 == 0 else 1
    padded = -(-rows // 128) * 128
    dma = pltpu.SemaphoreType.DMA
    vmem = pl.BlockSpec(memory_space=pltpu.VMEM)
    return pl.pallas_call(
        functools.partial(kernel, n_group, n_hold, capacity),
        out_shape=jax.ShapeDtypeStruct((block, width), BF16),
        in_specs=[vmem] * 7,
        out_specs=vmem,
        scratch_shapes=[
            pltpu.VMEM((experts_here, width, 2 * ff), BF16),
            pltpu.VMEM((width, experts_here * ff), BF16),
            pltpu.VMEM((n_hold, block, width), BF16),
            pltpu.VMEM((n_hold, 8, block), F32),
            pltpu.VMEM((n_hold, 8, block), F32),
            pltpu.VMEM((n_hold * block, experts_here * ff), BF16),
            pltpu.VMEM((n_hold, parts, block, width // parts), BF16),
            pltpu.VMEM((n_hold, parts, block, width // parts), BF16),
            pltpu.VMEM((128, 128), F32),
            pltpu.VMEM((ff, padded), F32),
            dma((experts_here * halves, 2 * chips)),
            dma((experts_here * halves, 2 * chips)),
            dma((halves, 2 * chips)),
            dma((halves, 2 * chips)),
            dma((n_hold,)),
            dma((n_hold,)),
            dma((n_hold,)),
            dma((n_hold,)),
            dma((n_hold, parts)),
            dma((n_hold, parts)),
        ],
        compiler_params=pltpu.CompilerParams(
            collective_id=0, has_side_effects=True, vmem_limit_bytes=56 * 2**20
        ),
    )(tokens, gate, up, down, routes, scores, live.reshape(1, block))


def solution(mesh):
    in_specs = (
        P(("group", "expert"), None),
        P("expert", "group", None),
        P("expert", "group", None),
        P("expert", None, "group"),
        P(("group", "expert"), None),
        P(("group", "expert"), None),
        P(("group", "expert")),
    )
    out_specs = P(("group", "expert"), None)
    body = functools.partial(local, mesh.shape["group"], mesh.shape["expert"])
    return jax.shard_map(body, mesh=mesh, in_specs=in_specs, out_specs=out_specs, check_vma=False)
```

```python
import functools

import jax
import jax.numpy as jnp
from jax import lax
from jax.experimental import pallas as pl
from jax.experimental.pallas import tpu as pltpu
from jax.sharding import PartitionSpec as P

MESH = pl.DeviceIdType.MESH
F32, BF16 = jnp.float32, jnp.bfloat16
PAIR = (((1,), (1,)), ((), ()))


def xor(value, mask):
    bit = 1
    while bit <= mask:
        if mask & bit:
            value = value + bit * (1 - 2 * ((value // bit) % 2))
        bit *= 2
    return value


def kernel(
    n_group, n_hold, capacity,
    tokens, gate, up, down, routes, scores, live, out,
    w_gu, w_down, tok_all, share_out, share_in, hidden, stage, back, flip, relay, ahead,
    gu_send, gu_recv, down_send, down_recv, tok_send, tok_recv, share_send, share_recv,
    ret_send, ret_recv, relay_send, relay_recv,
):
    local, rows, ff = gate.shape
    block, width = tokens.shape
    top = routes.shape[0]
    experts = local * n_hold
    chips = n_group // 2
    square = chips == 4
    me, holder = lax.axis_index("group"), lax.axis_index("expert")
    chip = me // 2
    sibling = xor(me, 1)

    def device(group, expert):
        return (group, expert)

    line = n_hold == 4
    order = (0, 2, 1, 3) if line else tuple(range(n_hold))
    at_low, at_high = holder == 0, holder == n_hold - 1
    inner = jnp.logical_not(jnp.logical_or(at_low, at_high))

    def peer(d):
        return lax.rem(holder + d, n_hold)

    def origin(d):
        return lax.rem(holder + n_hold - d, n_hold)

    near = (1, 2) if square else tuple(range(1, chips))
    barrier = pltpu.get_barrier_semaphore()
    partners = [device(xor(me, 2 * j), holder) for j in near] + [device(sibling, holder)]
    partners += [device(me, peer(d)) for d in range(1, n_hold)]
    for partner in partners:
        pl.semaphore_signal(barrier, inc=1, device_id=partner, device_id_type=MESH)

    mine = pl.multiple_of(me * rows, rows)

    def round_gate_up(e):
        w_gu[e, pl.ds(mine, rows), :ff] = gate[e].astype(BF16)
        w_gu[e, pl.ds(mine, rows), ff:] = up[e].astype(BF16)

    round_gate_up(0)
    pl.semaphore_wait(barrier, len(partners))

    started = []

    def start(src, dst, send, recv, target, when=None):
        copy = pltpu.make_async_remote_copy(
            src_ref=src, dst_ref=dst, send_sem=send, recv_sem=recv,
            device_id=target, device_id_type=MESH,
        )
        started.append((copy, when))
        if when is None:
            copy.start()
        else:
            pl.when(when)(copy.start)

    halves = 2 if square else 1
    half_rows = rows // halves

    def piece(kind, key, owner):
        base = pl.multiple_of(owner * rows + key[-1] * half_rows, half_rows)
        if kind == "gu":
            return w_gu.at[key[0], pl.ds(base, half_rows), :]
        return w_down.at[pl.ds(base, half_rows), :]

    def sems(kind, key):
        if kind == "gu":
            index = key[0] * halves + key[1]
            return gu_send, gu_recv, index
        return down_send, down_recv, key[0]

    def send_piece(kind, key, owner, slot, target):
        send, recv, index = sems(kind, key)
        ref = piece(kind, key, owner)
        start(ref, ref, send.at[index, slot], recv.at[index, slot], device(target, holder))

    def wait_piece(kind, key, owner, slot):
        send, recv, index = sems(kind, key)
        ref = piece(kind, key, owner)
        pltpu.make_async_remote_copy(
            src_ref=ref, dst_ref=ref, send_sem=send.at[index, slot], recv_sem=recv.at[index, slot],
            device_id=device(sibling, holder), device_id_type=MESH,
        ).wait_recv()

    def send_own(kind, keys):
        for key in keys:
            for j in near if key[-1] == 0 else near[::-1]:
                send_piece(kind, key, me, j, xor(me, 2 * j))
        for key in keys:
            send_piece(kind, key, me, chips, sibling)

    def service_near(kind, keys):
        for key in keys:
            for j in near:
                owner = xor(me, 2 * j)
                wait_piece(kind, key, owner, j)
                if square and (j == 1) == (key[-1] == 0):
                    send_piece(kind, key, owner, 3, xor(me, 2 * (3 - j)))
                send_piece(kind, key, owner, chips + j, sibling)

    def service_far(kind, keys):
        if square:
            for key in keys:
                owner = xor(me, 6)
                wait_piece(kind, key, owner, 3)
                send_piece(kind, key, owner, chips + 3, sibling)

    def wait_sibling(kind, keys, j):
        for key in keys:
            wait_piece(kind, key, xor(sibling, 2 * j), chips + j)

    gu_keys = [[(e, a) for a in range(halves)] for e in range(local)]
    down_keys = [(a,) for a in range(halves)]

    send_own("gu", gu_keys[0])
    for i in range(1, n_hold):
        d, when = order[i], None
        if line and d != 2:
            when = jnp.logical_not(at_high if d == 1 else at_low)
        start(tokens, tok_all.at[i], tok_send.at[i], tok_recv.at[i], device(me, peer(d)), when)
    for e in range(1, local):
        round_gate_up(e)
        send_own("gu", gu_keys[e])

    named_expert = routes[...].astype(F32)
    chosen = scores[...]
    chosen = chosen / jnp.sum(chosen, axis=0, keepdims=True)
    expert_id = lax.broadcasted_iota(jnp.int32, (experts, block), 0).astype(F32)
    weight = jnp.zeros((experts, block), F32)
    named = jnp.zeros((experts, block), F32)
    for k in range(top):
        hit = named_expert[k:k + 1] == expert_id
        weight = weight + jnp.where(hit, chosen[k:k + 1], 0.0)
        named = named + jnp.where(hit, 1.0, 0.0)
    alive = (live[...] > 0).astype(F32)
    named = named * alive
    before = (
        lax.broadcasted_iota(jnp.int32, (block, block), 0)
        < lax.broadcasted_iota(jnp.int32, (block, block), 1)
    ).astype(BF16)
    earlier = jnp.dot(named.astype(BF16), before, preferred_element_type=F32)
    weight = jnp.where((earlier < capacity) & (alive > 0), weight, 0.0)
    share_out[...] = jnp.zeros_like(share_out)
    for p in range(n_hold):
        share_out[p, :local, :] = weight[p * local:(p + 1) * local]
    for i in range(1, n_hold):
        start(
            share_out.at[peer(order[i])], share_in.at[i], share_send.at[i], share_recv.at[i],
            device(me, peer(order[i])),
        )

    for e in range(local):
        w_down[pl.ds(mine, rows), e * ff:(e + 1) * ff] = down[e].astype(BF16)
    tok_all[0] = tokens[...]
    share_in[0] = share_out[holder]
    flip[...] = jnp.zeros_like(flip)
    if line:
        @pl.when(at_high)
        def _():
            back[order.index(1)] = jnp.zeros(back.shape[1:], BF16)

        @pl.when(at_low)
        def _():
            back[order.index(3)] = jnp.zeros(back.shape[1:], BF16)

    def arrive(dst, recv):
        pltpu.make_async_remote_copy(
            src_ref=dst, dst_ref=dst, send_sem=recv, recv_sem=recv,
            device_id=device(sibling, holder), device_id_type=MESH,
        ).wait_recv()

    for e in range(local):
        service_near("gu", gu_keys[e])
        if line and e == 0:
            pl.when(inner)(lambda: arrive(tok_all.at[1], tok_recv.at[1]))
            slot = jnp.where(holder == 2, 3, 2)
            start(
                tok_all.at[1], tok_all.at[slot], tok_send.at[0], tok_recv.at[slot],
                device(me, jnp.where(holder == 2, 3, 0)), inner,
            )
        if e > 0:
            service_far("gu", gu_keys[e - 1])
    send_own("down", down_keys)
    service_far("gu", gu_keys[local - 1])
    for e in range(local):
        for j in range(chips):
            wait_sibling("gu", gu_keys[e], j)

    tile = 256
    per_group = 2

    def wait_tokens(i):
        if line and i == 1:
            pl.when(jnp.logical_not(inner))(lambda: arrive(tok_all.at[1], tok_recv.at[1]))
        else:
            arrive(tok_all.at[i], tok_recv.at[i])
        arrive(share_in.at[i], share_recv.at[i])

    def hidden_group(first):
        count = per_group * block
        flip[: per_group * 8] = share_in[first:first + per_group].reshape(per_group * 8, block)
        columns = flip[...].T
        picked = tok_all[first:first + per_group].reshape(count, width)
        for e in range(local):
            scale = jnp.concatenate(
                [columns[:, i * 8 + e:i * 8 + e + 1] for i in range(per_group)], axis=0
            )

            def body(j, carry):
                at = pl.multiple_of(j * tile, tile)
                g = jnp.dot(picked, w_gu[e, :, pl.ds(at, tile)], preferred_element_type=F32)
                u = jnp.dot(
                    picked, w_gu[e, :, pl.ds(pl.multiple_of(ff + at, tile), tile)],
                    preferred_element_type=F32,
                )
                value = (g / (1.0 + jnp.exp(-g))) * u * scale
                hidden[first * block:first * block + count,
                       pl.ds(pl.multiple_of(e * ff + at, tile), tile)] = value.astype(BF16)
                return carry

            lax.fori_loop(0, ff // tile, body, 0)

    for first in range(0, n_hold, per_group):
        if first == per_group or n_hold == per_group:
            service_near("down", down_keys)
        for d in range(first, first + per_group):
            if d > 0:
                wait_tokens(d)
        hidden_group(first)

    parts, piece_width = back.shape[1], back.shape[3]

    def column(part):
        if parts == 1:
            return 0
        return pl.multiple_of(xor(chip, part) * piece_width, piece_width)

    def send_back(i, part, when=None):
        start(
            stage.at[i, part], back.at[i, part],
            ret_send.at[i, part], ret_recv.at[i, part],
            device(me, origin(order[i])), when,
        )

    def pass_on(part):
        @pl.when(inner)
        def _():
            arrive(relay.at[part], relay_recv.at[part])
            stage[1, part] = (ahead[part % 2] + relay[part].astype(F32)).astype(BF16)
        send_back(1, part, inner)

    for part in range(parts):
        if parts == 1:
            service_far("down", down_keys)
            for j in range(chips):
                wait_sibling("down", down_keys, j)
        else:
            if part == min(2, parts - 1):
                service_far("down", down_keys)
            wait_sibling("down", down_keys, part)
        at = column(part)
        for first in range(0, n_hold, 4):
            count = min(4, n_hold - first)
            value = lax.dot_general(
                hidden[first * block:(first + count) * block, :],
                w_down[pl.ds(at, piece_width), :], PAIR, preferred_element_type=F32,
            )
            stage[first:first + count, part] = value.astype(BF16).reshape(
                count, block, piece_width
            )
            if line:
                ahead[part % 2] = value[block:2 * block]
        if line:
            far = jnp.where(at_low, 2, 3)
            start(
                stage.at[far, part], relay.at[part], relay_send.at[part], relay_recv.at[part],
                device(me, jnp.where(at_low, 1, 2)), jnp.logical_not(inner),
            )
            send_back(1, part, jnp.logical_not(inner))
            send_back(2, part, jnp.logical_not(at_low))
            send_back(3, part, jnp.logical_not(at_high))
            if part > 0:
                pass_on(part - 1)
            if part == parts - 1:
                pass_on(part)
        else:
            for i in range(n_hold - 1, 0, -1):
                send_back(i, part)

    for part in range(parts):
        total = stage[0, part].astype(F32)
        for i in range(1, n_hold):
            def landed(i=i, part=part):
                arrive(back.at[i, part], ret_recv.at[i, part])
            if line and i > 1:
                pl.when(jnp.logical_not(at_high if order[i] == 1 else at_low))(landed)
            else:
                landed()
            total = total + back[i, part].astype(F32)
        out[:, pl.ds(column(part), piece_width)] = total.astype(BF16)

    for copy, when in started:
        if when is None:
            copy.wait_send()
        else:
            pl.when(when)(copy.wait_send)


def local(n_group, n_hold, tokens, gate, up, down, routes, scores, live):
    experts_here, rows, ff = gate.shape
    block, width = tokens.shape
    down, routes, scores = jnp.swapaxes(down, 1, 2), routes.T, scores.T
    top = routes.shape[0]
    capacity = block * top // (experts_here * n_hold)
    chips = n_group // 2
    halves = 2 if chips == 4 else 1
    parts = chips if (2 * rows) % 128 == 0 else 1
    dma = pltpu.SemaphoreType.DMA
    vmem = pl.BlockSpec(memory_space=pltpu.VMEM)
    return pl.pallas_call(
        functools.partial(kernel, n_group, n_hold, capacity),
        out_shape=jax.ShapeDtypeStruct((block, width), BF16),
        in_specs=[vmem] * 7,
        out_specs=vmem,
        scratch_shapes=[
            pltpu.VMEM((experts_here, width, 2 * ff), BF16),
            pltpu.VMEM((width, experts_here * ff), BF16),
            pltpu.VMEM((n_hold, block, width), BF16),
            pltpu.VMEM((n_hold, 8, block), F32),
            pltpu.VMEM((n_hold, 8, block), F32),
            pltpu.VMEM((n_hold * block, experts_here * ff), BF16),
            pltpu.VMEM((n_hold, parts, block, width // parts), BF16),
            pltpu.VMEM((n_hold, parts, block, width // parts), BF16),
            pltpu.VMEM((128, 128), F32),
            pltpu.VMEM((parts, block, width // parts), BF16),
            pltpu.VMEM((2, block, width // parts), F32),
            dma((experts_here * halves, 2 * chips)),
            dma((experts_here * halves, 2 * chips)),
            dma((halves, 2 * chips)),
            dma((halves, 2 * chips)),
            dma((n_hold,)),
            dma((n_hold,)),
            dma((n_hold,)),
            dma((n_hold,)),
            dma((n_hold, parts)),
            dma((n_hold, parts)),
            dma((parts,)),
            dma((parts,)),
        ],
        compiler_params=pltpu.CompilerParams(
            collective_id=0, has_side_effects=True, vmem_limit_bytes=56 * 2**20
        ),
    )(tokens, gate, up, down, routes, scores, live.reshape(1, block))


def solution(mesh):
    in_specs = (
        P(("group", "expert"), None),
        P("expert", "group", None),
        P("expert", "group", None),
        P("expert", None, "group"),
        P(("group", "expert"), None),
        P(("group", "expert"), None),
        P(("group", "expert")),
    )
    out_specs = P(("group", "expert"), None)
    body = functools.partial(local, mesh.shape["group"], mesh.shape["expert"])
    return jax.shard_map(body, mesh=mesh, in_specs=in_specs, out_specs=out_specs, check_vma=False)
```

```python
import functools

import jax
import jax.numpy as jnp
from jax import lax
from jax.experimental import pallas as pl
from jax.experimental.pallas import tpu as pltpu
from jax.sharding import PartitionSpec as P

MESH = pl.DeviceIdType.MESH
F32, BF16 = jnp.float32, jnp.bfloat16
PAIR = (((1,), (1,)), ((), ()))


def xor(value, mask):
    bit = 1
    while bit <= mask:
        if mask & bit:
            value = value + bit * (1 - 2 * ((value // bit) % 2))
        bit *= 2
    return value


def kernel(
    n_group, n_hold, capacity,
    tokens_in, gate_in, up_in, down_in, routes, scores, live, out,
    gate, up, down, load, w_gu, w_down, tok_all, share_out, share_in, hidden, stage, back, flip, relay, ahead,
    gu_send, gu_recv, down_send, down_recv, tok_send, tok_recv, share_send, share_recv,
    ret_send, ret_recv, relay_send, relay_recv, hand_send, hand_recv,
):
    local, rows, ff = gate.shape
    block, width = tokens_in.shape
    top = routes.shape[0]
    experts = local * n_hold
    chips = n_group // 2
    square = chips == 4
    me, holder = lax.axis_index("group"), lax.axis_index("expert")
    chip = me // 2
    sibling = xor(me, 1)

    def device(group, expert):
        return (group, expert)

    line = n_hold == 4
    order = (0, 2, 1, 3) if line else tuple(range(n_hold))
    at_low, at_high = holder == 0, holder == n_hold - 1
    inner = jnp.logical_not(jnp.logical_or(at_low, at_high))

    def peer(d):
        return lax.rem(holder + d, n_hold)

    def origin(d):
        return lax.rem(holder + n_hold - d, n_hold)

    near = (1, 2) if square else tuple(range(1, chips))
    barrier = pltpu.get_barrier_semaphore()
    partners = [device(xor(me, 2 * j), holder) for j in near] + [device(sibling, holder)]
    partners += [device(me, peer(d)) for d in range(1, n_hold)]
    loads = {}
    tokens = tok_all.at[0]
    for number, (name, src, dst) in enumerate(
        [("gate0", gate_in.at[0], gate.at[0]), ("up0", up_in.at[0], up.at[0])]
        + [("tokens", tokens_in, tokens)]
        + [(name + str(e), src.at[e], dst.at[e]) for e in range(1, local) for name, src, dst in
           (("gate", gate_in, gate), ("up", up_in, up))]
        + [("down", down_in, down)]
    ):
        loads[name] = pltpu.make_async_copy(src, dst, load.at[number])
        loads[name].start()
    for partner in partners:
        pl.semaphore_signal(barrier, inc=1, device_id=partner, device_id_type=MESH)

    mine = pl.multiple_of(me * rows, rows)

    def round_gate_up(e):
        loads["gate" + str(e)].wait()
        loads["up" + str(e)].wait()
        w_gu[e, pl.ds(mine, rows), :ff] = gate[e].astype(BF16)
        w_gu[e, pl.ds(mine, rows), ff:] = up[e].astype(BF16)

    round_gate_up(0)
    pl.semaphore_wait(barrier, len(partners))

    started = []

    def start(src, dst, send, recv, target, when=None):
        copy = pltpu.make_async_remote_copy(
            src_ref=src, dst_ref=dst, send_sem=send, recv_sem=recv,
            device_id=target, device_id_type=MESH,
        )
        started.append((copy, when))
        if when is None:
            copy.start()
        else:
            pl.when(when)(copy.start)

    halves = 2 if square else 1
    half_rows = rows // halves

    def piece(kind, key, owner):
        base = pl.multiple_of(owner * rows + key[-1] * half_rows, half_rows)
        if kind == "gu":
            return w_gu.at[key[0], pl.ds(base, half_rows), :]
        return w_down.at[pl.ds(base, half_rows), :]

    def sems(kind, key):
        if kind == "gu":
            index = key[0] * halves + key[1]
            return gu_send, gu_recv, index
        return down_send, down_recv, key[0]

    def send_piece(kind, key, owner, slot, target):
        send, recv, index = sems(kind, key)
        ref = piece(kind, key, owner)
        start(ref, ref, send.at[index, slot], recv.at[index, slot], device(target, holder))

    def wait_piece(kind, key, owner, slot):
        send, recv, index = sems(kind, key)
        ref = piece(kind, key, owner)
        pltpu.make_async_remote_copy(
            src_ref=ref, dst_ref=ref, send_sem=send.at[index, slot], recv_sem=recv.at[index, slot],
            device_id=device(sibling, holder), device_id_type=MESH,
        ).wait_recv()

    def turns(keys):
        if not square:
            return [(key, j) for key in keys for j in near]
        return [(keys[0], 1), (keys[1], 2), (keys[1], 1), (keys[0], 2)]

    def send_own(kind, some):
        for key, j in some:
            send_piece(kind, key, me, j, xor(me, 2 * j))

    def send_core(kind, keys):
        for key in keys:
            send_piece(kind, key, me, chips, sibling)

    def service_near(kind, some):
        for key, j in some:
            owner = xor(me, 2 * j)
            wait_piece(kind, key, owner, j)
            if square and (j == 1) == (key[-1] == 0):
                send_piece(kind, key, owner, 3, xor(me, 2 * (3 - j)))
            send_piece(kind, key, owner, chips + j, sibling)

    def service_far(kind, keys):
        if square:
            for key in keys:
                owner = xor(me, 6)
                wait_piece(kind, key, owner, 3)
                send_piece(kind, key, owner, chips + 3, sibling)

    def wait_sibling(kind, keys, j):
        for key in keys:
            wait_piece(kind, key, xor(sibling, 2 * j), chips + j)

    gu_keys = [[(e, a) for a in range(halves)] for e in range(local)]
    down_keys = [(a,) for a in range(halves)]

    def half_block(i, half):
        return tok_all.at[i, pl.ds(half * (block // 2), block // 2), :]

    def send_tokens(i):
        d, when = order[i], None
        if line and d != 2:
            when = jnp.logical_not(at_high if d == 1 else at_low)
        start(tokens, tok_all.at[i], tok_send.at[i], tok_recv.at[i], device(me, peer(d)), when)

    first_turns = turns(gu_keys[0])
    send_own("gu", first_turns[:2])
    loads["tokens"].wait()
    if line:
        for half in range(2):
            start(
                half_block(0, half), half_block(1, half), hand_send.at[half], hand_recv.at[half],
                device(me, peer(2)),
            )
    send_own("gu", first_turns[2:])
    for i in range(2 if line else 1, n_hold):
        send_tokens(i)
    for e in range(1, local):
        round_gate_up(e)
        send_own("gu", turns(gu_keys[e]))
    for e in range(local):
        send_core("gu", gu_keys[e])

    named_expert = routes[...].astype(F32)
    chosen = scores[...]
    chosen = chosen / jnp.sum(chosen, axis=0, keepdims=True)
    expert_id = lax.broadcasted_iota(jnp.int32, (experts, block), 0).astype(F32)
    weight = jnp.zeros((experts, block), F32)
    named = jnp.zeros((experts, block), F32)
    for k in range(top):
        hit = named_expert[k:k + 1] == expert_id
        weight = weight + jnp.where(hit, chosen[k:k + 1], 0.0)
        named = named + jnp.where(hit, 1.0, 0.0)
    alive = (live[...] > 0).astype(F32)
    named = named * alive
    before = (
        lax.broadcasted_iota(jnp.int32, (block, block), 0)
        < lax.broadcasted_iota(jnp.int32, (block, block), 1)
    ).astype(BF16)
    earlier = jnp.dot(named.astype(BF16), before, preferred_element_type=F32)
    weight = jnp.where((earlier < capacity) & (alive > 0), weight, 0.0)
    share_out[...] = jnp.zeros_like(share_out)
    for p in range(n_hold):
        share_out[p, :local, :] = weight[p * local:(p + 1) * local]
    for i in range(1, n_hold):
        start(
            share_out.at[peer(order[i])], share_in.at[i], share_send.at[i], share_recv.at[i],
            device(me, peer(order[i])),
        )

    loads["down"].wait()
    for e in range(local):
        w_down[pl.ds(mine, rows), e * ff:(e + 1) * ff] = down[e].astype(BF16)
    share_in[0] = share_out[holder]
    flip[...] = jnp.zeros_like(flip)
    if line:
        @pl.when(at_high)
        def _():
            back[order.index(1)] = jnp.zeros(back.shape[1:], BF16)

        @pl.when(at_low)
        def _():
            back[order.index(3)] = jnp.zeros(back.shape[1:], BF16)

    def arrive(dst, recv):
        pltpu.make_async_remote_copy(
            src_ref=dst, dst_ref=dst, send_sem=recv, recv_sem=recv,
            device_id=device(sibling, holder), device_id_type=MESH,
        ).wait_recv()

    far_slot = jnp.where(holder == 2, 3, 2)
    far_end = jnp.where(holder == 2, 3, 0)

    def hand_on(half):
        if line:
            arrive(half_block(1, half), hand_recv.at[half])
            start(
                half_block(1, half), half_block(far_slot, half),
                hand_send.at[2 + half], hand_recv.at[2 + half], device(me, far_end), inner,
            )

    for e in range(local):
        some = turns(gu_keys[e])
        if e == 0:
            service_near("gu", some)
            hand_on(0)
        elif e == 1:
            service_near("gu", some[:2])
            hand_on(1)
            service_near("gu", some[2:])
        else:
            service_near("gu", some)
        if e < local - 1:
            service_far("gu", gu_keys[e])
    send_own("down", turns(down_keys))
    send_core("down", down_keys)

    tile = 256
    per_group = 2

    def wait_tokens(i):
        if line and i > 1:
            from_end = at_high if order[i] == 3 else at_low

            @pl.when(from_end)
            def _():
                for half in range(2):
                    arrive(half_block(i, half), hand_recv.at[2 + half])

            pl.when(jnp.logical_not(from_end))(lambda: arrive(tok_all.at[i], tok_recv.at[i]))
        elif not line:
            arrive(tok_all.at[i], tok_recv.at[i])
        arrive(share_in.at[i], share_recv.at[i])

    def hidden_group(first, e):
        count = per_group * block
        flip[: per_group * 8] = share_in[first:first + per_group].reshape(per_group * 8, block)
        columns = flip[...].T
        picked = tok_all[first:first + per_group].reshape(count, width)
        scale = jnp.concatenate(
            [columns[:, i * 8 + e:i * 8 + e + 1] for i in range(per_group)], axis=0
        )

        def body(j, carry):
            at = pl.multiple_of(j * tile, tile)
            g = jnp.dot(picked, w_gu[e, :, pl.ds(at, tile)], preferred_element_type=F32)
            u = jnp.dot(
                picked, w_gu[e, :, pl.ds(pl.multiple_of(ff + at, tile), tile)],
                preferred_element_type=F32,
            )
            value = (g / (1.0 + jnp.exp(-g))) * u * scale
            hidden[first * block:first * block + count,
                   pl.ds(pl.multiple_of(e * ff + at, tile), tile)] = value.astype(BF16)
            return carry

        lax.fori_loop(0, ff // tile, body, 0)

    wait_tokens(1)
    for e in range(local):
        if e == local - 1:
            service_far("gu", gu_keys[e])
        for j in range(chips):
            wait_sibling("gu", gu_keys[e], j)
        hidden_group(0, e)
    service_near("down", turns(down_keys))
    for first in range(per_group, n_hold, per_group):
        for i in range(first, first + per_group):
            wait_tokens(i)
        for e in range(local):
            hidden_group(first, e)

    parts, piece_width = back.shape[1], back.shape[3]

    def column(part):
        if parts == 1:
            return 0
        return pl.multiple_of(xor(chip, part) * piece_width, piece_width)

    def send_back(i, part, when=None):
        start(
            stage.at[i, part], back.at[i, part],
            ret_send.at[i, part], ret_recv.at[i, part],
            device(me, origin(order[i])), when,
        )

    def pass_on(part):
        @pl.when(inner)
        def _():
            arrive(relay.at[part], relay_recv.at[part])
            stage[1, part] = (ahead[part % 2] + relay[part].astype(F32)).astype(BF16)
        send_back(1, part, inner)

    for part in range(parts):
        if parts == 1:
            service_far("down", down_keys)
            for j in range(chips):
                wait_sibling("down", down_keys, j)
        else:
            if part == min(2, parts - 1):
                service_far("down", down_keys)
            wait_sibling("down", down_keys, part)
        at = column(part)
        for first in range(0, n_hold, 4):
            count = min(4, n_hold - first)
            value = lax.dot_general(
                hidden[first * block:(first + count) * block, :],
                w_down[pl.ds(at, piece_width), :], PAIR, preferred_element_type=F32,
            )
            stage[first:first + count, part] = value.astype(BF16).reshape(
                count, block, piece_width
            )
            if line:
                ahead[part % 2] = value[block:2 * block]
        if line:
            far = jnp.where(at_low, 2, 3)
            start(
                stage.at[far, part], relay.at[part], relay_send.at[part], relay_recv.at[part],
                device(me, jnp.where(at_low, 1, 2)), jnp.logical_not(inner),
            )
            send_back(1, part, jnp.logical_not(inner))
            send_back(2, part, jnp.logical_not(at_low))
            send_back(3, part, jnp.logical_not(at_high))
            if part > 0:
                pass_on(part - 1)
            if part == parts - 1:
                pass_on(part)
        else:
            for i in range(n_hold - 1, 0, -1):
                send_back(i, part)

    for part in range(parts):
        total = stage[0, part].astype(F32)
        for i in range(1, n_hold):
            def landed(i=i, part=part):
                arrive(back.at[i, part], ret_recv.at[i, part])
            if line and i > 1:
                pl.when(jnp.logical_not(at_high if order[i] == 1 else at_low))(landed)
            else:
                landed()
            total = total + back[i, part].astype(F32)
        out[:, pl.ds(column(part), piece_width)] = total.astype(BF16)

    for copy, when in started:
        if when is None:
            copy.wait_send()
        else:
            pl.when(when)(copy.wait_send)


def local(n_group, n_hold, tokens, gate, up, down, routes, scores, live):
    experts_here, rows, ff = gate.shape
    block, width = tokens.shape
    down, routes, scores = jnp.swapaxes(down, 1, 2), routes.T, scores.T
    top = routes.shape[0]
    capacity = block * top // (experts_here * n_hold)
    chips = n_group // 2
    halves = 2 if chips == 4 else 1
    parts = chips if (2 * rows) % 128 == 0 else 1
    dma = pltpu.SemaphoreType.DMA
    vmem = pl.BlockSpec(memory_space=pltpu.VMEM)
    return pl.pallas_call(
        functools.partial(kernel, n_group, n_hold, capacity),
        out_shape=jax.ShapeDtypeStruct((block, width), BF16),
        in_specs=[pl.BlockSpec(memory_space=pl.ANY)] * 4 + [vmem] * 3,
        out_specs=vmem,
        scratch_shapes=[
            pltpu.VMEM(gate.shape, F32),
            pltpu.VMEM(up.shape, F32),
            pltpu.VMEM(down.shape, F32),
            dma((2 + 2 * experts_here,)),
            pltpu.VMEM((experts_here, width, 2 * ff), BF16),
            pltpu.VMEM((width, experts_here * ff), BF16),
            pltpu.VMEM((n_hold, block, width), BF16),
            pltpu.VMEM((n_hold, 8, block), F32),
            pltpu.VMEM((n_hold, 8, block), F32),
            pltpu.VMEM((n_hold * block, experts_here * ff), BF16),
            pltpu.VMEM((n_hold, parts, block, width // parts), BF16),
            pltpu.VMEM((n_hold, parts, block, width // parts), BF16),
            pltpu.VMEM((128, 128), F32),
            pltpu.VMEM((parts, block, width // parts), BF16),
            pltpu.VMEM((2, block, width // parts), F32),
            dma((experts_here * halves, 2 * chips)),
            dma((experts_here * halves, 2 * chips)),
            dma((halves, 2 * chips)),
            dma((halves, 2 * chips)),
            dma((n_hold,)),
            dma((n_hold,)),
            dma((n_hold,)),
            dma((n_hold,)),
            dma((n_hold, parts)),
            dma((n_hold, parts)),
            dma((parts,)),
            dma((parts,)),
            dma((4,)),
            dma((4,)),
        ],
        compiler_params=pltpu.CompilerParams(
            collective_id=0, has_side_effects=True, vmem_limit_bytes=56 * 2**20
        ),
    )(tokens, gate, up, down, routes, scores, live.reshape(1, block))


def solution(mesh):
    in_specs = (
        P(("group", "expert"), None),
        P("expert", "group", None),
        P("expert", "group", None),
        P("expert", None, "group"),
        P(("group", "expert"), None),
        P(("group", "expert"), None),
        P(("group", "expert")),
    )
    out_specs = P(("group", "expert"), None)
    body = functools.partial(local, mesh.shape["group"], mesh.shape["expert"])
    return jax.shard_map(body, mesh=mesh, in_specs=in_specs, out_specs=out_specs, check_vma=False)
```

```python
import functools

import jax
import jax.numpy as jnp
from jax import lax
from jax.experimental import pallas as pl
from jax.experimental.pallas import tpu as pltpu
from jax.sharding import PartitionSpec as P

MESH = pl.DeviceIdType.MESH
F32, BF16 = jnp.float32, jnp.bfloat16
PAIR = (((1,), (1,)), ((), ()))


def xor(value, mask):
    bit = 1
    while bit <= mask:
        if mask & bit:
            value = value + bit * (1 - 2 * ((value // bit) % 2))
        bit *= 2
    return value


def kernel(
    n_group, n_hold, capacity,
    tokens_in, gate_in, up_in, down_in, routes, scores, live, out,
    gate, up, down, load, w_gu, w_down, tok_all, share_out, share_in, hidden, stage, back, flip, relay, ahead,
    gu_send, gu_recv, down_send, down_recv, tok_send, tok_recv, share_send, share_recv,
    ret_send, ret_recv, relay_send, relay_recv, hand_send, hand_recv,
):
    local, rows, ff = gate.shape
    block, width = tokens_in.shape
    top = routes.shape[0]
    experts = local * n_hold
    chips = n_group // 2
    square = chips == 4
    me, holder = lax.axis_index("group"), lax.axis_index("expert")
    chip = me // 2
    sibling = xor(me, 1)

    def device(group, expert):
        return (group, expert)

    line = n_hold == 4 and square and rows % 64 == 0
    order = (0, 2, 1, 3) if line else tuple(range(n_hold))
    at_low, at_high = holder == 0, holder == n_hold - 1
    inner = jnp.logical_not(jnp.logical_or(at_low, at_high))

    def peer(d):
        return lax.rem(holder + d, n_hold)

    def origin(d):
        return lax.rem(holder + n_hold - d, n_hold)

    near = (1, 2) if square else tuple(range(1, chips))
    barrier = pltpu.get_barrier_semaphore()
    partners = [device(xor(me, 2 * j), holder) for j in near] + [device(sibling, holder)]
    partners += [device(me, peer(d)) for d in range(1, n_hold)]
    loads = {}
    tokens = tok_all.at[0]
    for number, (name, src, dst) in enumerate(
        [("gate0", gate_in.at[0], gate.at[0]), ("up0", up_in.at[0], up.at[0])]
        + [("tokens", tokens_in, tokens)]
        + [(name + str(e), src.at[e], dst.at[e]) for e in range(1, local) for name, src, dst in
           (("gate", gate_in, gate), ("up", up_in, up))]
        + [("down", down_in, down)]
    ):
        loads[name] = pltpu.make_async_copy(src, dst, load.at[number])
        loads[name].start()
    for partner in partners:
        pl.semaphore_signal(barrier, inc=1, device_id=partner, device_id_type=MESH)

    mine = pl.multiple_of(me * rows, rows)

    def round_gate_up(e):
        loads["gate" + str(e)].wait()
        loads["up" + str(e)].wait()
        w_gu[e, pl.ds(mine, rows), :ff] = gate[e].astype(BF16)
        w_gu[e, pl.ds(mine, rows), ff:] = up[e].astype(BF16)

    round_gate_up(0)
    pl.semaphore_wait(barrier, len(partners))

    started = []

    def start(src, dst, send, recv, target, when=None):
        copy = pltpu.make_async_remote_copy(
            src_ref=src, dst_ref=dst, send_sem=send, recv_sem=recv,
            device_id=target, device_id_type=MESH,
        )
        started.append((copy, when))
        if when is None:
            copy.start()
        else:
            pl.when(when)(copy.start)

    halves = 2 if square else 1
    half_rows = rows // halves

    def piece(kind, key, owner):
        base = pl.multiple_of(owner * rows + key[-1] * half_rows, half_rows)
        if kind == "gu":
            return w_gu.at[key[0], pl.ds(base, half_rows), :]
        return w_down.at[pl.ds(base, half_rows), :]

    def sems(kind, key):
        if kind == "gu":
            index = key[0] * halves + key[1]
            return gu_send, gu_recv, index
        return down_send, down_recv, key[0]

    def send_piece(kind, key, owner, slot, target):
        send, recv, index = sems(kind, key)
        ref = piece(kind, key, owner)
        start(ref, ref, send.at[index, slot], recv.at[index, slot], device(target, holder))

    def wait_piece(kind, key, owner, slot):
        send, recv, index = sems(kind, key)
        ref = piece(kind, key, owner)
        pltpu.make_async_remote_copy(
            src_ref=ref, dst_ref=ref, send_sem=send.at[index, slot], recv_sem=recv.at[index, slot],
            device_id=device(sibling, holder), device_id_type=MESH,
        ).wait_recv()

    def turns(keys):
        if not square:
            return [(key, j) for key in keys for j in near]
        return [(keys[0], 1), (keys[1], 2), (keys[1], 1), (keys[0], 2)]

    def send_own(kind, some):
        for key, j in some:
            send_piece(kind, key, me, j, xor(me, 2 * j))

    def send_core(kind, keys):
        for key in keys:
            send_piece(kind, key, me, chips, sibling)

    def service_near(kind, some):
        for key, j in some:
            owner = xor(me, 2 * j)
            wait_piece(kind, key, owner, j)
            if square and (j == 1) == (key[-1] == 0):
                send_piece(kind, key, owner, 3, xor(me, 2 * (3 - j)))
            send_piece(kind, key, owner, chips + j, sibling)

    def service_far(kind, keys):
        if square:
            for key in keys:
                owner = xor(me, 6)
                wait_piece(kind, key, owner, 3)
                send_piece(kind, key, owner, chips + 3, sibling)

    def wait_sibling(kind, keys, j):
        for key in keys:
            wait_piece(kind, key, xor(sibling, 2 * j), chips + j)

    gu_keys = [[(e, a) for a in range(halves)] for e in range(local)]
    down_keys = [(a,) for a in range(halves)]

    def half_block(i, half):
        return tok_all.at[i, pl.ds(half * (block // 2), block // 2), :]

    def send_tokens(i):
        d, when = order[i], None
        if line and d != 2:
            when = jnp.logical_not(at_high if d == 1 else at_low)
        start(tokens, tok_all.at[i], tok_send.at[i], tok_recv.at[i], device(me, peer(d)), when)

    first_turns = turns(gu_keys[0])
    send_own("gu", first_turns[:2])
    loads["tokens"].wait()
    if line:
        for half in range(2):
            start(
                half_block(0, half), half_block(1, half), hand_send.at[half], hand_recv.at[half],
                device(me, peer(2)),
            )
    send_own("gu", first_turns[2:])
    for i in range(2 if line else 1, n_hold):
        send_tokens(i)
    for e in range(1, local):
        round_gate_up(e)
        send_own("gu", turns(gu_keys[e]))
    for e in range(local):
        send_core("gu", gu_keys[e])

    named_expert = routes[...].astype(F32)
    chosen = scores[...]
    chosen = chosen / jnp.sum(chosen, axis=0, keepdims=True)
    expert_id = lax.broadcasted_iota(jnp.int32, (experts, block), 0).astype(F32)
    weight = jnp.zeros((experts, block), F32)
    named = jnp.zeros((experts, block), F32)
    for k in range(top):
        hit = named_expert[k:k + 1] == expert_id
        weight = weight + jnp.where(hit, chosen[k:k + 1], 0.0)
        named = named + jnp.where(hit, 1.0, 0.0)
    alive = (live[...] > 0).astype(F32)
    named = named * alive
    before = (
        lax.broadcasted_iota(jnp.int32, (block, block), 0)
        < lax.broadcasted_iota(jnp.int32, (block, block), 1)
    ).astype(BF16)
    earlier = jnp.dot(named.astype(BF16), before, preferred_element_type=F32)
    weight = jnp.where((earlier < capacity) & (alive > 0), weight, 0.0)
    share_out[...] = jnp.zeros_like(share_out)
    for p in range(n_hold):
        share_out[p, :local, :] = weight[p * local:(p + 1) * local]
    for i in range(1, n_hold):
        start(
            share_out.at[peer(order[i])], share_in.at[i], share_send.at[i], share_recv.at[i],
            device(me, peer(order[i])),
        )

    loads["down"].wait()
    for e in range(local):
        w_down[pl.ds(mine, rows), e * ff:(e + 1) * ff] = down[e].astype(BF16)
    share_in[0] = share_out[holder]
    flip[...] = jnp.zeros_like(flip)
    if line:
        @pl.when(at_high)
        def _():
            back[order.index(1)] = jnp.zeros(back.shape[1:], BF16)

        @pl.when(at_low)
        def _():
            back[order.index(3)] = jnp.zeros(back.shape[1:], BF16)

    def arrive(dst, recv):
        pltpu.make_async_remote_copy(
            src_ref=dst, dst_ref=dst, send_sem=recv, recv_sem=recv,
            device_id=device(sibling, holder), device_id_type=MESH,
        ).wait_recv()

    far_slot = jnp.where(holder == 2, 3, 2)
    far_end = jnp.where(holder == 2, 3, 0)

    def hand_on(half):
        if line:
            arrive(half_block(1, half), hand_recv.at[half])
            start(
                half_block(1, half), half_block(far_slot, half),
                hand_send.at[2 + half], hand_recv.at[2 + half], device(me, far_end), inner,
            )

    for e in range(local):
        some = turns(gu_keys[e])
        if e == 0:
            service_near("gu", some)
            hand_on(0)
        elif e == 1:
            service_near("gu", some[:2])
            hand_on(1)
            service_near("gu", some[2:])
        else:
            service_near("gu", some)
        if e < local - 1:
            service_far("gu", gu_keys[e])
    send_own("down", turns(down_keys))
    send_core("down", down_keys)

    tile = 256
    per_group = 2

    def wait_tokens(i):
        if line and i > 1:
            from_end = at_high if order[i] == 3 else at_low

            @pl.when(from_end)
            def _():
                for half in range(2):
                    arrive(half_block(i, half), hand_recv.at[2 + half])

            pl.when(jnp.logical_not(from_end))(lambda: arrive(tok_all.at[i], tok_recv.at[i]))
        elif not line:
            arrive(tok_all.at[i], tok_recv.at[i])
        arrive(share_in.at[i], share_recv.at[i])

    def hidden_group(first, e):
        count = per_group * block
        flip[: per_group * 8] = share_in[first:first + per_group].reshape(per_group * 8, block)
        columns = flip[...].T
        picked = tok_all[first:first + per_group].reshape(count, width)
        scale = jnp.concatenate(
            [columns[:, i * 8 + e:i * 8 + e + 1] for i in range(per_group)], axis=0
        )

        def body(j, carry):
            at = pl.multiple_of(j * tile, tile)
            g = jnp.dot(picked, w_gu[e, :, pl.ds(at, tile)], preferred_element_type=F32)
            u = jnp.dot(
                picked, w_gu[e, :, pl.ds(pl.multiple_of(ff + at, tile), tile)],
                preferred_element_type=F32,
            )
            value = (g / (1.0 + jnp.exp(-g))) * u * scale
            hidden[first * block:first * block + count,
                   pl.ds(pl.multiple_of(e * ff + at, tile), tile)] = value.astype(BF16)
            return carry

        lax.fori_loop(0, ff // tile, body, 0)

    parts, piece_width = back.shape[1], back.shape[3]

    def column(part):
        if parts == 1:
            return 0
        return pl.multiple_of(xor(chip, part) * piece_width, piece_width)

    def send_back(i, part, when=None):
        start(
            stage.at[i, part], back.at[i, part],
            ret_send.at[i, part], ret_recv.at[i, part],
            device(me, origin(order[i])), when,
        )

    def pass_on(part):
        @pl.when(inner)
        def _():
            arrive(relay.at[part], relay_recv.at[part])
            stage[1, part] = (ahead[part % 2] + relay[part].astype(F32)).astype(BF16)
        send_back(1, part, inner)

    def rows_out(part, first, count):
        at = column(part)
        value = lax.dot_general(
            hidden[first * block:(first + count) * block, :],
            w_down[pl.ds(at, piece_width), :], PAIR, preferred_element_type=F32,
        )
        stage[first:first + count, part] = value.astype(BF16).reshape(count, block, piece_width)
        if line and first == 0:
            ahead[part % 2] = value[block:2 * block]

    def send_relay(part):
        far = jnp.where(at_low, 2, 3)
        start(
            stage.at[far, part], relay.at[part], relay_send.at[part], relay_recv.at[part],
            device(me, jnp.where(at_low, 1, 2)), jnp.logical_not(inner),
        )

    def send_near(part):
        send_back(2, part, jnp.logical_not(at_low))
        send_back(3, part, jnp.logical_not(at_high))

    if line:
        wait_tokens(1)
        for e in range(local):
            last = e == local - 1
            if last:
                service_far("gu", gu_keys[e])
            for j in range(chips):
                if not last:
                    wait_sibling("gu", gu_keys[e], j)
            if not last:
                hidden_group(0, e)
        for i in range(2, n_hold):
            wait_tokens(i)
        for e in range(local - 1):
            hidden_group(2, e)
        for j in range(chips):
            wait_sibling("gu", gu_keys[local - 1], j)
        hidden_group(0, local - 1)
        wait_sibling("down", down_keys, 0)
        rows_out(0, 0, 2)
        send_back(1, 0, jnp.logical_not(inner))
        hidden_group(2, local - 1)
        rows_out(0, 2, 2)
        send_relay(0)
        send_near(0)
        down_turns = turns(down_keys)
        service_near("down", down_turns[:2])
        pass_on(0)
        service_near("down", down_turns[2:])
        for part in range(1, parts):
            if part == parts - 1:
                service_far("down", down_keys)
            wait_sibling("down", down_keys, part)
            rows_out(part, 0, n_hold)
            send_relay(part)
            send_back(1, part, jnp.logical_not(inner))
            send_near(part)
            if part > 1:
                pass_on(part - 1)
        pass_on(parts - 1)
    else:
        for e in range(local):
            if e == local - 1:
                service_far("gu", gu_keys[e])
            for j in range(chips):
                wait_sibling("gu", gu_keys[e], j)
        service_near("down", turns(down_keys))
        service_far("down", down_keys)
        for j in range(chips):
            wait_sibling("down", down_keys, j)
        for i in range(1, n_hold):
            wait_tokens(i)
        for first in range(0, n_hold, per_group):
            for e in range(local):
                hidden_group(first, e)
            for part in range(parts):
                rows_out(part, first, per_group)
                for i in range(first, first + per_group):
                    if i > 0:
                        send_back(i, part)

    for part in range(parts):
        total = stage[0, part].astype(F32)
        for i in range(1, n_hold):
            def landed(i=i, part=part):
                arrive(back.at[i, part], ret_recv.at[i, part])
            if line and i > 1:
                pl.when(jnp.logical_not(at_high if order[i] == 1 else at_low))(landed)
            else:
                landed()
            total = total + back[i, part].astype(F32)
        out[:, pl.ds(column(part), piece_width)] = total.astype(BF16)

    for copy, when in started:
        if when is None:
            copy.wait_send()
        else:
            pl.when(when)(copy.wait_send)


def local(n_group, n_hold, tokens, gate, up, down, routes, scores, live):
    experts_here, rows, ff = gate.shape
    block, width = tokens.shape
    down, routes, scores = jnp.swapaxes(down, 1, 2), routes.T, scores.T
    top = routes.shape[0]
    capacity = block * top // (experts_here * n_hold)
    chips = n_group // 2
    halves = 2 if chips == 4 else 1
    parts = chips if (2 * rows) % 128 == 0 else 1
    dma = pltpu.SemaphoreType.DMA
    vmem = pl.BlockSpec(memory_space=pltpu.VMEM)
    return pl.pallas_call(
        functools.partial(kernel, n_group, n_hold, capacity),
        out_shape=jax.ShapeDtypeStruct((block, width), BF16),
        in_specs=[pl.BlockSpec(memory_space=pl.ANY)] * 4 + [vmem] * 3,
        out_specs=vmem,
        scratch_shapes=[
            pltpu.VMEM(gate.shape, F32),
            pltpu.VMEM(up.shape, F32),
            pltpu.VMEM(down.shape, F32),
            dma((2 + 2 * experts_here,)),
            pltpu.VMEM((experts_here, width, 2 * ff), BF16),
            pltpu.VMEM((width, experts_here * ff), BF16),
            pltpu.VMEM((n_hold, block, width), BF16),
            pltpu.VMEM((n_hold, 8, block), F32),
            pltpu.VMEM((n_hold, 8, block), F32),
            pltpu.VMEM((n_hold * block, experts_here * ff), BF16),
            pltpu.VMEM((n_hold, parts, block, width // parts), BF16),
            pltpu.VMEM((n_hold, parts, block, width // parts), BF16),
            pltpu.VMEM((128, 128), F32),
            pltpu.VMEM((parts, block, width // parts), BF16),
            pltpu.VMEM((2, block, width // parts), F32),
            dma((experts_here * halves, 2 * chips)),
            dma((experts_here * halves, 2 * chips)),
            dma((halves, 2 * chips)),
            dma((halves, 2 * chips)),
            dma((n_hold,)),
            dma((n_hold,)),
            dma((n_hold,)),
            dma((n_hold,)),
            dma((n_hold, parts)),
            dma((n_hold, parts)),
            dma((parts,)),
            dma((parts,)),
            dma((4,)),
            dma((4,)),
        ],
        compiler_params=pltpu.CompilerParams(
            collective_id=0, has_side_effects=True, vmem_limit_bytes=56 * 2**20
        ),
    )(tokens, gate, up, down, routes, scores, live.reshape(1, block))


def solution(mesh):
    in_specs = (
        P(("group", "expert"), None),
        P("expert", "group", None),
        P("expert", "group", None),
        P("expert", None, "group"),
        P(("group", "expert"), None),
        P(("group", "expert"), None),
        P(("group", "expert")),
    )
    out_specs = P(("group", "expert"), None)
    body = functools.partial(local, mesh.shape["group"], mesh.shape["expert"])
    return jax.shard_map(body, mesh=mesh, in_specs=in_specs, out_specs=out_specs, check_vma=False)
```

```python
import functools

import jax
import jax.numpy as jnp
from jax import lax
from jax.experimental import pallas as pl
from jax.experimental.pallas import tpu as pltpu
from jax.sharding import PartitionSpec as P

MESH = pl.DeviceIdType.MESH
F32, BF16 = jnp.float32, jnp.bfloat16
PAIR = (((1,), (1,)), ((), ()))


def xor(value, mask):
    bit = 1
    while bit <= mask:
        if mask & bit:
            value = value + bit * (1 - 2 * ((value // bit) % 2))
        bit *= 2
    return value


def kernel(
    n_group, n_hold, capacity,
    tokens_in, gate_in, up_in, down_in, routes, scores, live, out,
    gate, up, down, load, w_gu, w_down, tok_all, share_out, share_in, hidden, stage, back, flip, relay, ahead,
    gu_send, gu_recv, down_send, down_recv, tok_send, tok_recv, share_send, share_recv,
    ret_send, ret_recv, relay_send, relay_recv, hand_send, hand_recv,
):
    local, rows, ff = gate.shape
    block, width = tokens_in.shape
    top = routes.shape[0]
    experts = local * n_hold
    chips = n_group // 2
    square = chips == 4
    me, holder = lax.axis_index("group"), lax.axis_index("expert")
    chip = me // 2
    sibling = xor(me, 1)

    def device(group, expert):
        return (group, expert)

    line = n_hold == 4 and square and rows % 64 == 0
    order = (0, 2, 1, 3) if line else tuple(range(n_hold))
    at_low, at_high = holder == 0, holder == n_hold - 1
    inner = jnp.logical_not(jnp.logical_or(at_low, at_high))

    def peer(d):
        return lax.rem(holder + d, n_hold)

    def origin(d):
        return lax.rem(holder + n_hold - d, n_hold)

    near = (1, 2) if square else tuple(range(1, chips))
    barrier = pltpu.get_barrier_semaphore()
    partners = [device(xor(me, 2 * j), holder) for j in near] + [device(sibling, holder)]
    partners += [device(me, peer(d)) for d in range(1, n_hold)]
    loads = {}
    tokens = tok_all.at[0]
    for number, (name, src, dst) in enumerate(
        [("gate0", gate_in.at[0], gate.at[0]), ("up0", up_in.at[0], up.at[0])]
        + [("tokens", tokens_in, tokens)]
        + [(name + str(e), src.at[e], dst.at[e]) for e in range(1, local) for name, src, dst in
           (("gate", gate_in, gate), ("up", up_in, up))]
        + [("down", down_in, down)]
    ):
        loads[name] = pltpu.make_async_copy(src, dst, load.at[number])
        loads[name].start()
    for partner in partners:
        pl.semaphore_signal(barrier, inc=1, device_id=partner, device_id_type=MESH)

    mine = pl.multiple_of(me * rows, rows)

    def round_gate_up(e):
        loads["gate" + str(e)].wait()
        loads["up" + str(e)].wait()
        w_gu[e, pl.ds(mine, rows), :ff] = gate[e].astype(BF16)
        w_gu[e, pl.ds(mine, rows), ff:] = up[e].astype(BF16)

    round_gate_up(0)
    pl.semaphore_wait(barrier, len(partners))

    started = []

    def start(src, dst, send, recv, target, when=None):
        copy = pltpu.make_async_remote_copy(
            src_ref=src, dst_ref=dst, send_sem=send, recv_sem=recv,
            device_id=target, device_id_type=MESH,
        )
        started.append((copy, when))
        if when is None:
            copy.start()
        else:
            pl.when(when)(copy.start)

    halves = 2 if square else 1
    half_rows = rows // halves

    def piece(kind, key, owner):
        base = pl.multiple_of(owner * rows + key[-1] * half_rows, half_rows)
        if kind == "gu":
            return w_gu.at[key[0], pl.ds(base, half_rows), :]
        return w_down.at[pl.ds(base, half_rows), :]

    def sems(kind, key):
        if kind == "gu":
            index = key[0] * halves + key[1]
            return gu_send, gu_recv, index
        return down_send, down_recv, key[0]

    def send_piece(kind, key, owner, slot, target):
        send, recv, index = sems(kind, key)
        ref = piece(kind, key, owner)
        start(ref, ref, send.at[index, slot], recv.at[index, slot], device(target, holder))

    def wait_piece(kind, key, owner, slot):
        send, recv, index = sems(kind, key)
        ref = piece(kind, key, owner)
        pltpu.make_async_remote_copy(
            src_ref=ref, dst_ref=ref, send_sem=send.at[index, slot], recv_sem=recv.at[index, slot],
            device_id=device(sibling, holder), device_id_type=MESH,
        ).wait_recv()

    def turns(keys):
        if not square:
            return [(key, j) for key in keys for j in near]
        return [(keys[0], 1), (keys[1], 2), (keys[1], 1), (keys[0], 2)]

    def send_own(kind, some):
        for key, j in some:
            send_piece(kind, key, me, j, xor(me, 2 * j))

    def send_core(kind, keys):
        for key in keys:
            send_piece(kind, key, me, chips, sibling)

    def service_near(kind, some):
        for key, j in some:
            owner = xor(me, 2 * j)
            wait_piece(kind, key, owner, j)
            if square and (j == 1) == (key[-1] == 0):
                send_piece(kind, key, owner, 3, xor(me, 2 * (3 - j)))
            send_piece(kind, key, owner, chips + j, sibling)

    def service_far(kind, keys):
        if square:
            for key in keys:
                owner = xor(me, 6)
                wait_piece(kind, key, owner, 3)
                send_piece(kind, key, owner, chips + 3, sibling)

    def wait_sibling(kind, keys, j):
        for key in keys:
            wait_piece(kind, key, xor(sibling, 2 * j), chips + j)

    gu_keys = [[(e, a) for a in range(halves)] for e in range(local)]
    down_keys = [(a,) for a in range(halves)]

    def half_block(i, half):
        return tok_all.at[i, pl.ds(half * (block // 2), block // 2), :]

    def send_tokens(i):
        d, when = order[i], None
        if line and d != 2:
            when = jnp.logical_not(at_high if d == 1 else at_low)
        start(tokens, tok_all.at[i], tok_send.at[i], tok_recv.at[i], device(me, peer(d)), when)

    first_turns = turns(gu_keys[0])
    send_own("gu", first_turns[:2])
    loads["tokens"].wait()
    if line:
        for half in range(2):
            start(
                half_block(0, half), half_block(1, half), hand_send.at[half], hand_recv.at[half],
                device(me, peer(2)),
            )
    send_own("gu", first_turns[2:])
    for i in range(2 if line else 1, n_hold):
        send_tokens(i)
    for e in range(1, local):
        round_gate_up(e)
        send_own("gu", turns(gu_keys[e]))
    for e in range(local):
        send_core("gu", gu_keys[e])

    named_expert = routes[...].astype(F32)
    chosen = scores[...]
    chosen = chosen / jnp.sum(chosen, axis=0, keepdims=True)
    expert_id = lax.broadcasted_iota(jnp.int32, (experts, block), 0).astype(F32)
    weight = jnp.zeros((experts, block), F32)
    named = jnp.zeros((experts, block), F32)
    for k in range(top):
        hit = named_expert[k:k + 1] == expert_id
        weight = weight + jnp.where(hit, chosen[k:k + 1], 0.0)
        named = named + jnp.where(hit, 1.0, 0.0)
    alive = (live[...] > 0).astype(F32)
    named = named * alive
    before = (
        lax.broadcasted_iota(jnp.int32, (block, block), 0)
        < lax.broadcasted_iota(jnp.int32, (block, block), 1)
    ).astype(BF16)
    earlier = jnp.dot(named.astype(BF16), before, preferred_element_type=F32)
    weight = jnp.where((earlier < capacity) & (alive > 0), weight, 0.0)
    share_out[...] = jnp.zeros_like(share_out)
    for p in range(n_hold):
        share_out[p, :local, :] = weight[p * local:(p + 1) * local]
    for i in range(1, n_hold):
        start(
            share_out.at[peer(order[i])], share_in.at[i], share_send.at[i], share_recv.at[i],
            device(me, peer(order[i])),
        )

    loads["down"].wait()
    for e in range(local):
        w_down[pl.ds(mine, rows), e * ff:(e + 1) * ff] = down[e].astype(BF16)
    share_in[0] = share_out[holder]
    flip[...] = jnp.zeros_like(flip)
    if line:
        @pl.when(at_high)
        def _():
            back[order.index(1)] = jnp.zeros(back.shape[1:], BF16)

        @pl.when(at_low)
        def _():
            back[order.index(3)] = jnp.zeros(back.shape[1:], BF16)

    def arrive(dst, recv):
        pltpu.make_async_remote_copy(
            src_ref=dst, dst_ref=dst, send_sem=recv, recv_sem=recv,
            device_id=device(sibling, holder), device_id_type=MESH,
        ).wait_recv()

    far_slot = jnp.where(holder == 2, 3, 2)
    far_end = jnp.where(holder == 2, 3, 0)

    def hand_on(half):
        if line:
            arrive(half_block(1, half), hand_recv.at[half])
            start(
                half_block(1, half), half_block(far_slot, half),
                hand_send.at[2 + half], hand_recv.at[2 + half], device(me, far_end), inner,
            )

    for e in range(local):
        some = turns(gu_keys[e])
        if e == 0:
            service_near("gu", some)
            hand_on(0)
        elif e == 1:
            service_near("gu", some[:2])
            hand_on(1)
            service_near("gu", some[2:])
        else:
            service_near("gu", some)
        if e < local - 1:
            service_far("gu", gu_keys[e])
    send_core("down", down_keys)

    tile = 256
    per_group = 2

    def wait_tokens(i):
        if line and i > 1:
            from_end = at_high if order[i] == 3 else at_low

            @pl.when(from_end)
            def _():
                for half in range(2):
                    arrive(half_block(i, half), hand_recv.at[2 + half])

            pl.when(jnp.logical_not(from_end))(lambda: arrive(tok_all.at[i], tok_recv.at[i]))
        elif not line:
            arrive(tok_all.at[i], tok_recv.at[i])
        arrive(share_in.at[i], share_recv.at[i])

    def hidden_group(first, e):
        count = per_group * block
        flip[: per_group * 8] = share_in[first:first + per_group].reshape(per_group * 8, block)
        columns = flip[...].T
        picked = tok_all[first:first + per_group].reshape(count, width)
        scale = jnp.concatenate(
            [columns[:, i * 8 + e:i * 8 + e + 1] for i in range(per_group)], axis=0
        )

        def body(j, carry):
            at = pl.multiple_of(j * tile, tile)
            g = jnp.dot(picked, w_gu[e, :, pl.ds(at, tile)], preferred_element_type=F32)
            u = jnp.dot(
                picked, w_gu[e, :, pl.ds(pl.multiple_of(ff + at, tile), tile)],
                preferred_element_type=F32,
            )
            value = (g / (1.0 + jnp.exp(-g))) * u * scale
            hidden[first * block:first * block + count,
                   pl.ds(pl.multiple_of(e * ff + at, tile), tile)] = value.astype(BF16)
            return carry

        lax.fori_loop(0, ff // tile, body, 0)

    parts, piece_width = back.shape[1], back.shape[3]

    def column(part):
        if parts == 1:
            return 0
        return pl.multiple_of(xor(chip, part) * piece_width, piece_width)

    def send_back(i, part, when=None):
        start(
            stage.at[i, part], back.at[i, part],
            ret_send.at[i, part], ret_recv.at[i, part],
            device(me, origin(order[i])), when,
        )

    def pass_on(part):
        @pl.when(inner)
        def _():
            arrive(relay.at[part], relay_recv.at[part])
            stage[1, part] = (ahead[part % 2] + relay[part].astype(F32)).astype(BF16)
        send_back(1, part, inner)

    def rows_out(part, first, count):
        at = column(part)
        value = lax.dot_general(
            hidden[first * block:(first + count) * block, :],
            w_down[pl.ds(at, piece_width), :], PAIR, preferred_element_type=F32,
        )
        stage[first:first + count, part] = value.astype(BF16).reshape(count, block, piece_width)
        if line and first == 0:
            ahead[part % 2] = value[block:2 * block]

    def send_relay(part):
        far = jnp.where(at_low, 2, 3)
        start(
            stage.at[far, part], relay.at[part], relay_send.at[part], relay_recv.at[part],
            device(me, jnp.where(at_low, 1, 2)), jnp.logical_not(inner),
        )

    def send_near(part):
        send_back(2, part, jnp.logical_not(at_low))
        send_back(3, part, jnp.logical_not(at_high))

    if line:
        wait_tokens(1)
        for e in range(local):
            last = e == local - 1
            if last:
                service_far("gu", gu_keys[e])
                send_own("down", turns(down_keys))
            for j in range(chips):
                if not last:
                    wait_sibling("gu", gu_keys[e], j)
            if not last:
                hidden_group(0, e)
        for i in range(2, n_hold):
            wait_tokens(i)
        for e in range(local - 1):
            hidden_group(2, e)
        for j in range(chips):
            wait_sibling("gu", gu_keys[local - 1], j)
        hidden_group(0, local - 1)
        wait_sibling("down", down_keys, 0)
        rows_out(0, 0, 2)
        send_back(1, 0, jnp.logical_not(inner))
        hidden_group(2, local - 1)
        rows_out(0, 2, 2)
        send_relay(0)
        send_near(0)
        down_turns = turns(down_keys)
        service_near("down", down_turns[:2])
        pass_on(0)
        service_near("down", down_turns[2:])
        for part in range(1, parts):
            if part == parts - 1:
                service_far("down", down_keys)
            wait_sibling("down", down_keys, part)
            rows_out(part, 0, n_hold)
            send_relay(part)
            send_back(1, part, jnp.logical_not(inner))
            send_near(part)
            if part > 1:
                pass_on(part - 1)
        pass_on(parts - 1)
    else:
        for e in range(local):
            if e == local - 1:
                service_far("gu", gu_keys[e])
                send_own("down", turns(down_keys))
            for j in range(chips):
                wait_sibling("gu", gu_keys[e], j)
        service_near("down", turns(down_keys))
        service_far("down", down_keys)
        for j in range(chips):
            wait_sibling("down", down_keys, j)
        for i in range(1, n_hold):
            wait_tokens(i)
        for first in range(0, n_hold, per_group):
            for e in range(local):
                hidden_group(first, e)
            for part in range(parts):
                rows_out(part, first, per_group)
                for i in range(first, first + per_group):
                    if i > 0:
                        send_back(i, part)

    for part in range(parts):
        total = stage[0, part].astype(F32)
        for i in range(1, n_hold):
            def landed(i=i, part=part):
                arrive(back.at[i, part], ret_recv.at[i, part])
            if line and i > 1:
                pl.when(jnp.logical_not(at_high if order[i] == 1 else at_low))(landed)
            else:
                landed()
            total = total + back[i, part].astype(F32)
        out[:, pl.ds(column(part), piece_width)] = total.astype(BF16)

    for copy, when in started:
        if when is None:
            copy.wait_send()
        else:
            pl.when(when)(copy.wait_send)


def local(n_group, n_hold, tokens, gate, up, down, routes, scores, live):
    experts_here, rows, ff = gate.shape
    block, width = tokens.shape
    down, routes, scores = jnp.swapaxes(down, 1, 2), routes.T, scores.T
    top = routes.shape[0]
    capacity = block * top // (experts_here * n_hold)
    chips = n_group // 2
    halves = 2 if chips == 4 else 1
    parts = chips if (2 * rows) % 128 == 0 else 1
    dma = pltpu.SemaphoreType.DMA
    vmem = pl.BlockSpec(memory_space=pltpu.VMEM)
    return pl.pallas_call(
        functools.partial(kernel, n_group, n_hold, capacity),
        out_shape=pltpu.VMEM((block, width), BF16),
        in_specs=[pl.BlockSpec(memory_space=pl.ANY)] * 4 + [vmem] * 3,
        out_specs=vmem,
        scratch_shapes=[
            pltpu.VMEM(gate.shape, F32),
            pltpu.VMEM(up.shape, F32),
            pltpu.VMEM(down.shape, F32),
            dma((2 + 2 * experts_here,)),
            pltpu.VMEM((experts_here, width, 2 * ff), BF16),
            pltpu.VMEM((width, experts_here * ff), BF16),
            pltpu.VMEM((n_hold, block, width), BF16),
            pltpu.VMEM((n_hold, 8, block), F32),
            pltpu.VMEM((n_hold, 8, block), F32),
            pltpu.VMEM((n_hold * block, experts_here * ff), BF16),
            pltpu.VMEM((n_hold, parts, block, width // parts), BF16),
            pltpu.VMEM((n_hold, parts, block, width // parts), BF16),
            pltpu.VMEM((128, 128), F32),
            pltpu.VMEM((parts, block, width // parts), BF16),
            pltpu.VMEM((2, block, width // parts), F32),
            dma((experts_here * halves, 2 * chips)),
            dma((experts_here * halves, 2 * chips)),
            dma((halves, 2 * chips)),
            dma((halves, 2 * chips)),
            dma((n_hold,)),
            dma((n_hold,)),
            dma((n_hold,)),
            dma((n_hold,)),
            dma((n_hold, parts)),
            dma((n_hold, parts)),
            dma((parts,)),
            dma((parts,)),
            dma((4,)),
            dma((4,)),
        ],
        compiler_params=pltpu.CompilerParams(
            collective_id=0, has_side_effects=True, vmem_limit_bytes=52 * 2**20
        ),
    )(tokens, gate, up, down, routes, scores, live.reshape(1, block))


def solution(mesh):
    in_specs = (
        P(("group", "expert"), None),
        P("expert", "group", None),
        P("expert", "group", None),
        P("expert", None, "group"),
        P(("group", "expert"), None),
        P(("group", "expert"), None),
        P(("group", "expert")),
    )
    out_specs = P(("group", "expert"), None)
    body = functools.partial(local, mesh.shape["group"], mesh.shape["expert"])
    return jax.shard_map(body, mesh=mesh, in_specs=in_specs, out_specs=out_specs, check_vma=False)
```

```python
import functools

import jax
import jax.numpy as jnp
from jax import lax
from jax.experimental import pallas as pl
from jax.experimental.pallas import tpu as pltpu
from jax.sharding import PartitionSpec as P

MESH = pl.DeviceIdType.MESH
F32, BF16 = jnp.float32, jnp.bfloat16
PAIR = (((1,), (1,)), ((), ()))


def xor(value, mask):
    bit = 1
    while bit <= mask:
        if mask & bit:
            value = value + bit * (1 - 2 * ((value // bit) % 2))
        bit *= 2
    return value


def kernel(
    n_group, n_hold, capacity,
    tokens_in, gate_in, up_in, down_in, routes, scores, live, out,
    gate, up, down, load, w_gu, w_down, tok_all, share_out, share_in, hidden, stage, back, flip, relay, ahead,
    gu_send, gu_recv, down_send, down_recv, tok_send, tok_recv, share_send, share_recv,
    ret_send, ret_recv, relay_send, relay_recv, hand_send, hand_recv,
):
    local, rows, ff = gate.shape
    block, width = tokens_in.shape
    top = routes.shape[0]
    experts = local * n_hold
    chips = n_group // 2
    square = chips == 4
    me, holder = lax.axis_index("group"), lax.axis_index("expert")
    chip = me // 2
    sibling = xor(me, 1)

    def device(group, expert):
        return (group, expert)

    line = n_hold == 4 and square and rows % 64 == 0
    order = (0, 2, 1, 3) if line else tuple(range(n_hold))
    at_low, at_high = holder == 0, holder == n_hold - 1
    inner = jnp.logical_not(jnp.logical_or(at_low, at_high))

    def peer(d):
        return lax.rem(holder + d, n_hold)

    def origin(d):
        return lax.rem(holder + n_hold - d, n_hold)

    near = (1, 2) if square else tuple(range(1, chips))
    barrier = pltpu.get_barrier_semaphore()
    partners = [device(xor(me, 2 * j), holder) for j in near] + [device(sibling, holder)]
    partners += [device(me, peer(d)) for d in range(1, n_hold)]
    loads = {}
    tokens = tok_all.at[0]
    for number, (name, src, dst) in enumerate(
        [("gate0", gate_in.at[0], gate.at[0]), ("up0", up_in.at[0], up.at[0])]
        + [("tokens", tokens_in, tokens)]
        + [(name + str(e), src.at[e], dst.at[e]) for e in range(1, local) for name, src, dst in
           (("gate", gate_in, gate), ("up", up_in, up))]
        + [("down", down_in, down)]
    ):
        loads[name] = pltpu.make_async_copy(src, dst, load.at[number])
        loads[name].start()
    for partner in partners:
        pl.semaphore_signal(barrier, inc=1, device_id=partner, device_id_type=MESH)

    mine = pl.multiple_of(me * rows, rows)

    def round_gate_up(e):
        loads["gate" + str(e)].wait()
        loads["up" + str(e)].wait()
        w_gu[e, pl.ds(mine, rows), :ff] = gate[e].astype(BF16)
        w_gu[e, pl.ds(mine, rows), ff:] = up[e].astype(BF16)

    round_gate_up(0)
    pl.semaphore_wait(barrier, len(partners))

    started = []

    def start(src, dst, send, recv, target, when=None):
        copy = pltpu.make_async_remote_copy(
            src_ref=src, dst_ref=dst, send_sem=send, recv_sem=recv,
            device_id=target, device_id_type=MESH,
        )
        started.append((copy, when))
        if when is None:
            copy.start()
        else:
            pl.when(when)(copy.start)

    halves = 2 if square else 1
    half_rows = rows // halves

    def piece(kind, key, owner):
        base = pl.multiple_of(owner * rows + key[-1] * half_rows, half_rows)
        if kind == "gu":
            return w_gu.at[key[0], pl.ds(base, half_rows), :]
        return w_down.at[pl.ds(base, half_rows), :]

    def sems(kind, key):
        if kind == "gu":
            index = key[0] * halves + key[1]
            return gu_send, gu_recv, index
        return down_send, down_recv, key[0]

    def send_piece(kind, key, owner, slot, target):
        send, recv, index = sems(kind, key)
        ref = piece(kind, key, owner)
        start(ref, ref, send.at[index, slot], recv.at[index, slot], device(target, holder))

    def wait_piece(kind, key, owner, slot):
        send, recv, index = sems(kind, key)
        ref = piece(kind, key, owner)
        pltpu.make_async_remote_copy(
            src_ref=ref, dst_ref=ref, send_sem=send.at[index, slot], recv_sem=recv.at[index, slot],
            device_id=device(sibling, holder), device_id_type=MESH,
        ).wait_recv()

    def turns(keys):
        if not square:
            return [(key, j) for key in keys for j in near]
        return [(keys[0], 1), (keys[1], 2), (keys[1], 1), (keys[0], 2)]

    def send_own(kind, some):
        for key, j in some:
            send_piece(kind, key, me, j, xor(me, 2 * j))

    def send_core(kind, keys):
        for key in keys:
            send_piece(kind, key, me, chips, sibling)

    def service_near(kind, some):
        for key, j in some:
            owner = xor(me, 2 * j)
            wait_piece(kind, key, owner, j)
            if square and (j == 1) == (key[-1] == 0):
                send_piece(kind, key, owner, 3, xor(me, 2 * (3 - j)))
            send_piece(kind, key, owner, chips + j, sibling)

    def service_far(kind, keys):
        if square:
            for key in keys:
                owner = xor(me, 6)
                wait_piece(kind, key, owner, 3)
                send_piece(kind, key, owner, chips + 3, sibling)

    def wait_sibling(kind, keys, j):
        for key in keys:
            wait_piece(kind, key, xor(sibling, 2 * j), chips + j)

    gu_keys = [[(e, a) for a in range(halves)] for e in range(local)]
    down_keys = [(a,) for a in range(halves)]

    def half_block(i, half):
        return tok_all.at[i, pl.ds(half * (block // 2), block // 2), :]

    def send_tokens(i):
        d, when = order[i], None
        if line and d != 2:
            when = jnp.logical_not(at_high if d == 1 else at_low)
        start(tokens, tok_all.at[i], tok_send.at[i], tok_recv.at[i], device(me, peer(d)), when)

    first_turns = turns(gu_keys[0])
    send_own("gu", first_turns[:2])
    loads["tokens"].wait()
    if line:
        for half in range(2):
            start(
                half_block(0, half), half_block(1, half), hand_send.at[half], hand_recv.at[half],
                device(me, peer(2)),
            )
    send_own("gu", first_turns[2:])
    for i in range(2 if line else 1, n_hold):
        send_tokens(i)
    for e in range(1, local):
        round_gate_up(e)
        send_own("gu", turns(gu_keys[e]))
    for e in range(local):
        send_core("gu", gu_keys[e])

    named_expert = routes[...].astype(F32)
    chosen = scores[...]
    chosen = chosen / jnp.sum(chosen, axis=0, keepdims=True)
    expert_id = lax.broadcasted_iota(jnp.int32, (experts, block), 0).astype(F32)
    weight = jnp.zeros((experts, block), F32)
    named = jnp.zeros((experts, block), F32)
    for k in range(top):
        hit = named_expert[k:k + 1] == expert_id
        weight = weight + jnp.where(hit, chosen[k:k + 1], 0.0)
        named = named + jnp.where(hit, 1.0, 0.0)
    alive = (live[...] > 0).astype(F32)
    named = named * alive
    before = (
        lax.broadcasted_iota(jnp.int32, (block, block), 0)
        < lax.broadcasted_iota(jnp.int32, (block, block), 1)
    ).astype(BF16)
    earlier = jnp.dot(named.astype(BF16), before, preferred_element_type=F32)
    weight = jnp.where((earlier < capacity) & (alive > 0), weight, 0.0)
    share_out[...] = jnp.zeros_like(share_out)
    for p in range(n_hold):
        share_out[p, :local, :] = weight[p * local:(p + 1) * local]
    for i in range(1, n_hold):
        start(
            share_out.at[peer(order[i])], share_in.at[i], share_send.at[i], share_recv.at[i],
            device(me, peer(order[i])),
        )

    loads["down"].wait()
    for e in range(local):
        w_down[pl.ds(mine, rows), e * ff:(e + 1) * ff] = down[e].astype(BF16)
    share_in[0] = share_out[holder]
    flip[...] = jnp.zeros_like(flip)
    if line:
        @pl.when(at_high)
        def _():
            back[order.index(1)] = jnp.zeros(back.shape[1:], BF16)

        @pl.when(at_low)
        def _():
            back[order.index(3)] = jnp.zeros(back.shape[1:], BF16)

    def arrive(dst, recv):
        pltpu.make_async_remote_copy(
            src_ref=dst, dst_ref=dst, send_sem=recv, recv_sem=recv,
            device_id=device(sibling, holder), device_id_type=MESH,
        ).wait_recv()

    far_slot = jnp.where(holder == 2, 3, 2)
    far_end = jnp.where(holder == 2, 3, 0)

    def hand_on(half):
        if line:
            arrive(half_block(1, half), hand_recv.at[half])
            start(
                half_block(1, half), half_block(far_slot, half),
                hand_send.at[2 + half], hand_recv.at[2 + half], device(me, far_end), inner,
            )

    for e in range(local):
        some = turns(gu_keys[e])
        if e == 0:
            service_near("gu", some)
            hand_on(0)
        elif e == 1:
            service_near("gu", some[:2])
            hand_on(1)
            service_near("gu", some[2:])
        else:
            service_near("gu", some)
        if e < local - 1:
            service_far("gu", gu_keys[e])
    send_core("down", down_keys)

    tile = 256
    per_group = 2

    def wait_tokens(i):
        if line and i > 1:
            from_end = at_high if order[i] == 3 else at_low

            @pl.when(from_end)
            def _():
                for half in range(2):
                    arrive(half_block(i, half), hand_recv.at[2 + half])

            pl.when(jnp.logical_not(from_end))(lambda: arrive(tok_all.at[i], tok_recv.at[i]))
        elif not line:
            arrive(tok_all.at[i], tok_recv.at[i])
        arrive(share_in.at[i], share_recv.at[i])

    def hidden_group(first, e):
        count = per_group * block
        flip[: per_group * 8] = share_in[first:first + per_group].reshape(per_group * 8, block)
        columns = flip[...].T
        picked = tok_all[first:first + per_group].reshape(count, width)
        scale = jnp.concatenate(
            [columns[:, i * 8 + e:i * 8 + e + 1] for i in range(per_group)], axis=0
        )

        def body(j, carry):
            at = pl.multiple_of(j * tile, tile)
            g = jnp.dot(picked, w_gu[e, :, pl.ds(at, tile)], preferred_element_type=F32)
            u = jnp.dot(
                picked, w_gu[e, :, pl.ds(pl.multiple_of(ff + at, tile), tile)],
                preferred_element_type=F32,
            )
            value = (g / (1.0 + jnp.exp(-g))) * u * scale
            hidden[first * block:first * block + count,
                   pl.ds(pl.multiple_of(e * ff + at, tile), tile)] = value.astype(BF16)
            return carry

        lax.fori_loop(0, ff // tile, body, 0)

    parts, piece_width = back.shape[1], back.shape[3]

    def column(part):
        if parts == 1:
            return 0
        return pl.multiple_of(xor(chip, part) * piece_width, piece_width)

    def send_back(i, part, when=None):
        start(
            stage.at[i, part], back.at[i, part],
            ret_send.at[i, part], ret_recv.at[i, part],
            device(me, origin(order[i])), when,
        )

    def pass_on(part):
        @pl.when(inner)
        def _():
            arrive(relay.at[part], relay_recv.at[part])
            stage[1, part] = (ahead[part % 2] + relay[part].astype(F32)).astype(BF16)
        send_back(1, part, inner)

    def rows_out(part, first, count):
        at = column(part)
        value = lax.dot_general(
            hidden[first * block:(first + count) * block, :],
            w_down[pl.ds(at, piece_width), :], PAIR, preferred_element_type=F32,
        )
        stage[first:first + count, part] = value.astype(BF16).reshape(count, block, piece_width)
        if line and first == 0:
            ahead[part % 2] = value[block:2 * block]

    def send_relay(part):
        far = jnp.where(at_low, 2, 3)
        start(
            stage.at[far, part], relay.at[part], relay_send.at[part], relay_recv.at[part],
            device(me, jnp.where(at_low, 1, 2)), jnp.logical_not(inner),
        )

    def send_near(part):
        send_back(2, part, inner)
        send_back(3, part, inner)

    def send_near_end(part):
        send_back(2, part, at_high)
        send_back(3, part, at_low)

    if line:
        wait_tokens(1)
        for e in range(local):
            last = e == local - 1
            if last:
                service_far("gu", gu_keys[e])
                send_own("down", turns(down_keys))
            for j in range(chips):
                if not last:
                    wait_sibling("gu", gu_keys[e], j)
            if not last:
                hidden_group(0, e)
        for i in range(2, n_hold):
            wait_tokens(i)
        for e in range(local - 1):
            hidden_group(2, e)
        for j in range(chips):
            wait_sibling("gu", gu_keys[local - 1], j)
        hidden_group(0, local - 1)
        wait_sibling("down", down_keys, 0)
        rows_out(0, 0, 2)
        send_back(1, 0, jnp.logical_not(inner))
        hidden_group(2, local - 1)
        rows_out(0, 2, 2)
        send_relay(0)
        send_near(0)
        send_near_end(0)
        down_turns = turns(down_keys)
        service_near("down", down_turns[:2])
        pass_on(0)
        service_near("down", down_turns[2:])
        for part in range(1, parts):
            if part == parts - 1:
                service_far("down", down_keys)
            wait_sibling("down", down_keys, part)
            rows_out(part, 0, n_hold)
            send_relay(part)
            send_back(1, part, jnp.logical_not(inner))
            send_near(part)
            if part > 1:
                send_near_end(part - 1)
            if part == parts - 1:
                send_near_end(part)
            if part > 1:
                pass_on(part - 1)
        pass_on(parts - 1)
    else:
        for e in range(local):
            if e == local - 1:
                service_far("gu", gu_keys[e])
                send_own("down", turns(down_keys))
            for j in range(chips):
                wait_sibling("gu", gu_keys[e], j)
        service_near("down", turns(down_keys))
        service_far("down", down_keys)
        for j in range(chips):
            wait_sibling("down", down_keys, j)
        for i in range(1, n_hold):
            wait_tokens(i)
        for first in range(0, n_hold, per_group):
            for e in range(local):
                hidden_group(first, e)
            for part in range(parts):
                rows_out(part, first, per_group)
                for i in range(first, first + per_group):
                    if i > 0:
                        send_back(i, part)

    for part in range(parts):
        total = stage[0, part].astype(F32)
        for i in range(1, n_hold):
            def landed(i=i, part=part):
                arrive(back.at[i, part], ret_recv.at[i, part])
            if line and i > 1:
                pl.when(jnp.logical_not(at_high if order[i] == 1 else at_low))(landed)
            else:
                landed()
            total = total + back[i, part].astype(F32)
        out[:, pl.ds(column(part), piece_width)] = total.astype(BF16)

    for copy, when in started:
        if when is None:
            copy.wait_send()
        else:
            pl.when(when)(copy.wait_send)


def local(n_group, n_hold, tokens, gate, up, down, routes, scores, live):
    experts_here, rows, ff = gate.shape
    block, width = tokens.shape
    down, routes, scores = jnp.swapaxes(down, 1, 2), routes.T, scores.T
    top = routes.shape[0]
    capacity = block * top // (experts_here * n_hold)
    chips = n_group // 2
    halves = 2 if chips == 4 else 1
    parts = chips if (2 * rows) % 128 == 0 else 1
    dma = pltpu.SemaphoreType.DMA
    vmem = pl.BlockSpec(memory_space=pltpu.VMEM)
    return pl.pallas_call(
        functools.partial(kernel, n_group, n_hold, capacity),
        out_shape=pltpu.VMEM((block, width), BF16),
        in_specs=[pl.BlockSpec(memory_space=pltpu.HBM)] * 4 + [vmem] * 3,
        out_specs=vmem,
        scratch_shapes=[
            pltpu.VMEM(gate.shape, F32),
            pltpu.VMEM(up.shape, F32),
            pltpu.VMEM(down.shape, F32),
            dma((2 + 2 * experts_here,)),
            pltpu.VMEM((experts_here, width, 2 * ff), BF16),
            pltpu.VMEM((width, experts_here * ff), BF16),
            pltpu.VMEM((n_hold, block, width), BF16),
            pltpu.VMEM((n_hold, 8, block), F32),
            pltpu.VMEM((n_hold, 8, block), F32),
            pltpu.VMEM((n_hold * block, experts_here * ff), BF16),
            pltpu.VMEM((n_hold, parts, block, width // parts), BF16),
            pltpu.VMEM((n_hold, parts, block, width // parts), BF16),
            pltpu.VMEM((128, 128), F32),
            pltpu.VMEM((parts, block, width // parts), BF16),
            pltpu.VMEM((2, block, width // parts), F32),
            dma((experts_here * halves, 2 * chips)),
            dma((experts_here * halves, 2 * chips)),
            dma((halves, 2 * chips)),
            dma((halves, 2 * chips)),
            dma((n_hold,)),
            dma((n_hold,)),
            dma((n_hold,)),
            dma((n_hold,)),
            dma((n_hold, parts)),
            dma((n_hold, parts)),
            dma((parts,)),
            dma((parts,)),
            dma((4,)),
            dma((4,)),
        ],
        compiler_params=pltpu.CompilerParams(
            collective_id=0, has_side_effects=True, vmem_limit_bytes=58 * 2**20
        ),
    )(tokens, gate, up, down, routes, scores, live.reshape(1, block))


def solution(mesh):
    in_specs = (
        P(("group", "expert"), None),
        P("expert", "group", None),
        P("expert", "group", None),
        P("expert", None, "group"),
        P(("group", "expert"), None),
        P(("group", "expert"), None),
        P(("group", "expert")),
    )
    out_specs = P(("group", "expert"), None)
    body = functools.partial(local, mesh.shape["group"], mesh.shape["expert"])
    return jax.shard_map(body, mesh=mesh, in_specs=in_specs, out_specs=out_specs, check_vma=False)
```

```python
import functools

import jax
import jax.numpy as jnp
from jax import lax
from jax.experimental import pallas as pl
from jax.experimental.pallas import tpu as pltpu
from jax.sharding import PartitionSpec as P

MESH = pl.DeviceIdType.MESH
F32, BF16 = jnp.float32, jnp.bfloat16
PAIR = (((1,), (1,)), ((), ()))


def xor(value, mask):
    bit = 1
    while bit <= mask:
        if mask & bit:
            value = value + bit * (1 - 2 * ((value // bit) % 2))
        bit *= 2
    return value


def kernel(
    n_group, n_hold, capacity,
    tokens_in, gate_in, up_in, down_in, routes_in, scores_in, live_in, out,
    gate, up, down, routes, scores, live, load, w_gu, w_down, tok_all, share_out, share_in, hidden, stage, back, flip, relay, ahead,
    gu_send, gu_recv, down_send, down_recv, tok_send, tok_recv, share_send, share_recv,
    ret_send, ret_recv, relay_send, relay_recv, hand_send, hand_recv,
):
    local, rows, ff = gate.shape
    block, width = tokens_in.shape
    top = routes.shape[0]
    experts = local * n_hold
    chips = n_group // 2
    square = chips == 4
    me, holder = lax.axis_index("group"), lax.axis_index("expert")
    chip = me // 2
    sibling = xor(me, 1)

    def device(group, expert):
        return (group, expert)

    line = n_hold == 4 and square and rows % 64 == 0
    order = (0, 2, 1, 3) if line else tuple(range(n_hold))
    at_low, at_high = holder == 0, holder == n_hold - 1
    inner = jnp.logical_not(jnp.logical_or(at_low, at_high))

    def peer(d):
        return lax.rem(holder + d, n_hold)

    def origin(d):
        return lax.rem(holder + n_hold - d, n_hold)

    near = (1, 2) if square else tuple(range(1, chips))
    barrier = pltpu.get_barrier_semaphore()
    partners = [device(xor(me, 2 * j), holder) for j in near] + [device(sibling, holder)]
    partners += [device(me, peer(d)) for d in range(1, n_hold)]
    for partner in partners:
        pl.semaphore_signal(barrier, inc=1, device_id=partner, device_id_type=MESH)
    loads = {}
    tokens = tok_all.at[0]
    for number, (name, src, dst) in enumerate(
        [("gate0", gate_in.at[0], gate.at[0]), ("up0", up_in.at[0], up.at[0])]
        + [("tokens", tokens_in, tokens)]
        + [(name + str(e), src.at[e], dst.at[e]) for e in range(1, local) for name, src, dst in
           (("gate", gate_in, gate), ("up", up_in, up))]
        + [("routes", routes_in, routes), ("scores", scores_in, scores), ("live", live_in, live)]
        + [("down", down_in, down)]
    ):
        loads[name] = pltpu.make_async_copy(src, dst, load.at[number])
        loads[name].start()

    mine = pl.multiple_of(me * rows, rows)

    def round_gate_up(e):
        loads["gate" + str(e)].wait()
        loads["up" + str(e)].wait()
        w_gu[e, pl.ds(mine, rows), :ff] = gate[e].astype(BF16)
        w_gu[e, pl.ds(mine, rows), ff:] = up[e].astype(BF16)

    round_gate_up(0)
    pl.semaphore_wait(barrier, len(partners))

    started = []

    def start(src, dst, send, recv, target, when=None):
        copy = pltpu.make_async_remote_copy(
            src_ref=src, dst_ref=dst, send_sem=send, recv_sem=recv,
            device_id=target, device_id_type=MESH,
        )
        started.append((copy, when))
        if when is None:
            copy.start()
        else:
            pl.when(when)(copy.start)

    halves = 2 if square else 1
    half_rows = rows // halves

    def piece(kind, key, owner):
        base = pl.multiple_of(owner * rows + key[-1] * half_rows, half_rows)
        if kind == "gu":
            return w_gu.at[key[0], pl.ds(base, half_rows), :]
        return w_down.at[pl.ds(base, half_rows), :]

    def sems(kind, key):
        if kind == "gu":
            index = key[0] * halves + key[1]
            return gu_send, gu_recv, index
        return down_send, down_recv, key[0]

    def send_piece(kind, key, owner, slot, target):
        send, recv, index = sems(kind, key)
        ref = piece(kind, key, owner)
        start(ref, ref, send.at[index, slot], recv.at[index, slot], device(target, holder))

    def wait_piece(kind, key, owner, slot):
        send, recv, index = sems(kind, key)
        ref = piece(kind, key, owner)
        pltpu.make_async_remote_copy(
            src_ref=ref, dst_ref=ref, send_sem=send.at[index, slot], recv_sem=recv.at[index, slot],
            device_id=device(sibling, holder), device_id_type=MESH,
        ).wait_recv()

    def turns(keys):
        if not square:
            return [(key, j) for key in keys for j in near]
        return [(keys[0], 1), (keys[1], 2), (keys[1], 1), (keys[0], 2)]

    def send_own(kind, some):
        for key, j in some:
            send_piece(kind, key, me, j, xor(me, 2 * j))

    def send_core(kind, keys):
        for key in keys:
            send_piece(kind, key, me, chips, sibling)

    def service_near(kind, some):
        for key, j in some:
            owner = xor(me, 2 * j)
            wait_piece(kind, key, owner, j)
            if square and (j == 1) == (key[-1] == 0):
                send_piece(kind, key, owner, 3, xor(me, 2 * (3 - j)))
            send_piece(kind, key, owner, chips + j, sibling)

    def service_far(kind, keys):
        if square:
            for key in keys:
                owner = xor(me, 6)
                wait_piece(kind, key, owner, 3)
                send_piece(kind, key, owner, chips + 3, sibling)

    def wait_sibling(kind, keys, j):
        for key in keys:
            wait_piece(kind, key, xor(sibling, 2 * j), chips + j)

    gu_keys = [[(e, a) for a in range(halves)] for e in range(local)]
    down_keys = [(a,) for a in range(halves)]

    def half_block(i, half):
        return tok_all.at[i, pl.ds(half * (block // 2), block // 2), :]

    def send_tokens(i):
        d, when = order[i], None
        if line and d != 2:
            when = jnp.logical_not(at_high if d == 1 else at_low)
        start(tokens, tok_all.at[i], tok_send.at[i], tok_recv.at[i], device(me, peer(d)), when)

    first_turns = turns(gu_keys[0])
    send_own("gu", first_turns[:2])
    loads["tokens"].wait()
    if line:
        for half in range(2):
            start(
                half_block(0, half), half_block(1, half), hand_send.at[half], hand_recv.at[half],
                device(me, peer(2)),
            )
    send_own("gu", first_turns[2:])
    for i in range(2 if line else 1, n_hold):
        send_tokens(i)
    for e in range(1, local):
        round_gate_up(e)
        send_own("gu", turns(gu_keys[e]))
    for e in range(local):
        send_core("gu", gu_keys[e])

    for name in ("routes", "scores", "live"):
        loads[name].wait()
    named_expert = routes[...].astype(F32)
    chosen = scores[...]
    chosen = chosen / jnp.sum(chosen, axis=0, keepdims=True)
    expert_id = lax.broadcasted_iota(jnp.int32, (experts, block), 0).astype(F32)
    weight = jnp.zeros((experts, block), F32)
    named = jnp.zeros((experts, block), F32)
    for k in range(top):
        hit = named_expert[k:k + 1] == expert_id
        weight = weight + jnp.where(hit, chosen[k:k + 1], 0.0)
        named = named + jnp.where(hit, 1.0, 0.0)
    alive = (live[...] > 0).astype(F32)
    named = named * alive
    before = (
        lax.broadcasted_iota(jnp.int32, (block, block), 0)
        < lax.broadcasted_iota(jnp.int32, (block, block), 1)
    ).astype(BF16)
    earlier = jnp.dot(named.astype(BF16), before, preferred_element_type=F32)
    weight = jnp.where((earlier < capacity) & (alive > 0), weight, 0.0)
    share_out[...] = jnp.zeros_like(share_out)
    for p in range(n_hold):
        share_out[p, :local, :] = weight[p * local:(p + 1) * local]
    for i in range(1, n_hold):
        start(
            share_out.at[peer(order[i])], share_in.at[i], share_send.at[i], share_recv.at[i],
            device(me, peer(order[i])),
        )

    loads["down"].wait()
    for e in range(local):
        w_down[pl.ds(mine, rows), e * ff:(e + 1) * ff] = down[e].astype(BF16)
    share_in[0] = share_out[holder]
    flip[...] = jnp.zeros_like(flip)
    if line:
        @pl.when(at_high)
        def _():
            back[order.index(1)] = jnp.zeros(back.shape[1:], BF16)

        @pl.when(at_low)
        def _():
            back[order.index(3)] = jnp.zeros(back.shape[1:], BF16)

    def arrive(dst, recv):
        pltpu.make_async_remote_copy(
            src_ref=dst, dst_ref=dst, send_sem=recv, recv_sem=recv,
            device_id=device(sibling, holder), device_id_type=MESH,
        ).wait_recv()

    far_slot = jnp.where(holder == 2, 3, 2)
    far_end = jnp.where(holder == 2, 3, 0)

    def hand_on(half):
        if line:
            arrive(half_block(1, half), hand_recv.at[half])
            start(
                half_block(1, half), half_block(far_slot, half),
                hand_send.at[2 + half], hand_recv.at[2 + half], device(me, far_end), inner,
            )

    for e in range(local):
        some = turns(gu_keys[e])
        if e == 0:
            service_near("gu", some)
            hand_on(0)
        elif e == 1:
            service_near("gu", some[:2])
            hand_on(1)
            service_near("gu", some[2:])
        else:
            service_near("gu", some)
        if e < local - 1:
            service_far("gu", gu_keys[e])
    send_core("down", down_keys)

    tile = 256
    per_group = 2

    def wait_tokens(i):
        if line and i > 1:
            from_end = at_high if order[i] == 3 else at_low

            @pl.when(from_end)
            def _():
                for half in range(2):
                    arrive(half_block(i, half), hand_recv.at[2 + half])

            pl.when(jnp.logical_not(from_end))(lambda: arrive(tok_all.at[i], tok_recv.at[i]))
        elif not line:
            arrive(tok_all.at[i], tok_recv.at[i])
        arrive(share_in.at[i], share_recv.at[i])

    def hidden_group(first, e):
        count = per_group * block
        flip[: per_group * 8] = share_in[first:first + per_group].reshape(per_group * 8, block)
        columns = flip[...].T
        picked = tok_all[first:first + per_group].reshape(count, width)
        scale = jnp.concatenate(
            [columns[:, i * 8 + e:i * 8 + e + 1] for i in range(per_group)], axis=0
        )

        def body(j, carry):
            at = pl.multiple_of(j * tile, tile)
            g = jnp.dot(picked, w_gu[e, :, pl.ds(at, tile)], preferred_element_type=F32)
            u = jnp.dot(
                picked, w_gu[e, :, pl.ds(pl.multiple_of(ff + at, tile), tile)],
                preferred_element_type=F32,
            )
            value = (g / (1.0 + jnp.exp(-g))) * u * scale
            hidden[first * block:first * block + count,
                   pl.ds(pl.multiple_of(e * ff + at, tile), tile)] = value.astype(BF16)
            return carry

        lax.fori_loop(0, ff // tile, body, 0)

    parts, piece_width = back.shape[1], back.shape[3]

    def column(part):
        if parts == 1:
            return 0
        return pl.multiple_of(xor(chip, part) * piece_width, piece_width)

    def send_back(i, part, when=None):
        start(
            stage.at[i, part], back.at[i, part],
            ret_send.at[i, part], ret_recv.at[i, part],
            device(me, origin(order[i])), when,
        )

    def pass_on(part):
        @pl.when(inner)
        def _():
            arrive(relay.at[part], relay_recv.at[part])
            stage[1, part] = (ahead[part % 2] + relay[part].astype(F32)).astype(BF16)
        send_back(1, part, inner)

    def rows_out(part, first, count):
        at = column(part)
        value = lax.dot_general(
            hidden[first * block:(first + count) * block, :],
            w_down[pl.ds(at, piece_width), :], PAIR, preferred_element_type=F32,
        )
        stage[first:first + count, part] = value.astype(BF16).reshape(count, block, piece_width)
        if line and first == 0:
            ahead[part % 2] = value[block:2 * block]

    def send_relay(part):
        far = jnp.where(at_low, 2, 3)
        start(
            stage.at[far, part], relay.at[part], relay_send.at[part], relay_recv.at[part],
            device(me, jnp.where(at_low, 1, 2)), jnp.logical_not(inner),
        )

    def send_near(part):
        send_back(2, part, inner)
        send_back(3, part, inner)

    def send_near_end(part):
        send_back(2, part, at_high)
        send_back(3, part, at_low)

    if line:
        wait_tokens(1)
        for e in range(local):
            last = e == local - 1
            if last:
                service_far("gu", gu_keys[e])
                send_own("down", turns(down_keys))
            for j in range(chips):
                if not last:
                    wait_sibling("gu", gu_keys[e], j)
            if not last:
                hidden_group(0, e)
        for i in range(2, n_hold):
            wait_tokens(i)
        for e in range(local - 1):
            hidden_group(2, e)
        for j in range(chips):
            wait_sibling("gu", gu_keys[local - 1], j)
        hidden_group(2, local - 1)
        wait_sibling("down", down_keys, 0)
        rows_out(0, 2, 2)
        send_relay(0)
        send_near(0)
        send_near_end(0)
        hidden_group(0, local - 1)
        rows_out(0, 0, 2)
        send_back(1, 0, jnp.logical_not(inner))
        down_turns = turns(down_keys)
        service_near("down", down_turns[:2])
        pass_on(0)
        service_near("down", down_turns[2:])
        for part in range(1, parts):
            if part == parts - 1:
                service_far("down", down_keys)
            wait_sibling("down", down_keys, part)
            rows_out(part, 0, n_hold)
            send_relay(part)
            send_back(1, part, jnp.logical_not(inner))
            send_near(part)
            if part > 1:
                send_near_end(part - 1)
            if part == parts - 1:
                send_near_end(part)
            if part > 1:
                pass_on(part - 1)
        pass_on(parts - 1)
    else:
        for e in range(local):
            if e == local - 1:
                service_far("gu", gu_keys[e])
                send_own("down", turns(down_keys))
            for j in range(chips):
                wait_sibling("gu", gu_keys[e], j)
        service_near("down", turns(down_keys))
        service_far("down", down_keys)
        for j in range(chips):
            wait_sibling("down", down_keys, j)
        for i in range(1, n_hold):
            wait_tokens(i)
        for first in range(0, n_hold, per_group):
            for e in range(local):
                hidden_group(first, e)
            for part in range(parts):
                rows_out(part, first, per_group)
                for i in range(first, first + per_group):
                    if i > 0:
                        send_back(i, part)

    for part in range(parts):
        total = stage[0, part].astype(F32)
        for i in range(1, n_hold):
            def landed(i=i, part=part):
                arrive(back.at[i, part], ret_recv.at[i, part])
            if line and i > 1:
                pl.when(jnp.logical_not(at_high if order[i] == 1 else at_low))(landed)
            else:
                landed()
            total = total + back[i, part].astype(F32)
        out[:, pl.ds(column(part), piece_width)] = total.astype(BF16)

    for copy, when in started:
        if when is None:
            copy.wait_send()
        else:
            pl.when(when)(copy.wait_send)


def local(n_group, n_hold, tokens, gate, up, down, routes, scores, live):
    experts_here, rows, ff = gate.shape
    block, width = tokens.shape
    down, routes, scores = jnp.swapaxes(down, 1, 2), routes.T, scores.T
    top = routes.shape[0]
    capacity = block * top // (experts_here * n_hold)
    chips = n_group // 2
    halves = 2 if chips == 4 else 1
    parts = chips if (2 * rows) % 128 == 0 else 1
    dma = pltpu.SemaphoreType.DMA
    vmem = pl.BlockSpec(memory_space=pltpu.VMEM)
    return pl.pallas_call(
        functools.partial(kernel, n_group, n_hold, capacity),
        out_shape=pltpu.VMEM((block, width), BF16),
        in_specs=[pl.BlockSpec(memory_space=pltpu.HBM)] * 7,
        out_specs=vmem,
        scratch_shapes=[
            pltpu.VMEM(gate.shape, F32),
            pltpu.VMEM(up.shape, F32),
            pltpu.VMEM(down.shape, F32),
            pltpu.VMEM(routes.shape, jnp.int32),
            pltpu.VMEM(scores.shape, F32),
            pltpu.VMEM((1, block), jnp.int32),
            dma((5 + 2 * experts_here,)),
            pltpu.VMEM((experts_here, width, 2 * ff), BF16),
            pltpu.VMEM((width, experts_here * ff), BF16),
            pltpu.VMEM((n_hold, block, width), BF16),
            pltpu.VMEM((n_hold, 8, block), F32),
            pltpu.VMEM((n_hold, 8, block), F32),
            pltpu.VMEM((n_hold * block, experts_here * ff), BF16),
            pltpu.VMEM((n_hold, parts, block, width // parts), BF16),
            pltpu.VMEM((n_hold, parts, block, width // parts), BF16),
            pltpu.VMEM((128, 128), F32),
            pltpu.VMEM((parts, block, width // parts), BF16),
            pltpu.VMEM((2, block, width // parts), F32),
            dma((experts_here * halves, 2 * chips)),
            dma((experts_here * halves, 2 * chips)),
            dma((halves, 2 * chips)),
            dma((halves, 2 * chips)),
            dma((n_hold,)),
            dma((n_hold,)),
            dma((n_hold,)),
            dma((n_hold,)),
            dma((n_hold, parts)),
            dma((n_hold, parts)),
            dma((parts,)),
            dma((parts,)),
            dma((4,)),
            dma((4,)),
        ],
        compiler_params=pltpu.CompilerParams(
            collective_id=0, has_side_effects=True, vmem_limit_bytes=58 * 2**20
        ),
    )(tokens, gate, up, down, routes, scores, live.reshape(1, block))


def solution(mesh):
    in_specs = (
        P(("group", "expert"), None),
        P("expert", "group", None),
        P("expert", "group", None),
        P("expert", None, "group"),
        P(("group", "expert"), None),
        P(("group", "expert"), None),
        P(("group", "expert")),
    )
    out_specs = P(("group", "expert"), None)
    body = functools.partial(local, mesh.shape["group"], mesh.shape["expert"])
    return jax.shard_map(body, mesh=mesh, in_specs=in_specs, out_specs=out_specs, check_vma=False)
```

```python
import functools

import jax
import jax.numpy as jnp
from jax import lax
from jax.experimental import pallas as pl
from jax.experimental.pallas import tpu as pltpu
from jax.sharding import PartitionSpec as P

MESH = pl.DeviceIdType.MESH
F32, BF16 = jnp.float32, jnp.bfloat16
PAIR = (((1,), (1,)), ((), ()))


def xor(value, mask):
    bit = 1
    while bit <= mask:
        if mask & bit:
            value = value + bit * (1 - 2 * ((value // bit) % 2))
        bit *= 2
    return value


def kernel(
    n_group, n_hold, capacity,
    tokens_in, gate_in, up_in, down_in, routes_in, scores_in, live_in, out,
    gate, up, down, routes, scores, live, load, w_gu, w_down, tok_all, share_out, share_in, hidden, stage, back, flip, relay, ahead, early,
    gu_send, gu_recv, down_send, down_recv, tok_send, tok_recv, share_send, share_recv,
    ret_send, ret_recv, relay_send, relay_recv, hand_send, hand_recv,
):
    local, rows, ff = gate.shape
    block, width = tokens_in.shape
    top = routes.shape[0]
    experts = local * n_hold
    chips = n_group // 2
    square = chips == 4
    me, holder = lax.axis_index("group"), lax.axis_index("expert")
    chip = me // 2
    sibling = xor(me, 1)

    def device(group, expert):
        return (group, expert)

    line = n_hold == 4 and square and rows % 64 == 0
    order = (0, 2, 1, 3) if line else tuple(range(n_hold))
    at_low, at_high = holder == 0, holder == n_hold - 1
    inner = jnp.logical_not(jnp.logical_or(at_low, at_high))

    def peer(d):
        return lax.rem(holder + d, n_hold)

    def origin(d):
        return lax.rem(holder + n_hold - d, n_hold)

    near = (1, 2) if square else tuple(range(1, chips))
    barrier = pltpu.get_barrier_semaphore()
    partners = [device(xor(me, 2 * j), holder) for j in near] + [device(sibling, holder)]
    partners += [device(me, peer(d)) for d in range(1, n_hold)]
    for partner in partners:
        pl.semaphore_signal(barrier, inc=1, device_id=partner, device_id_type=MESH)
    loads = {}
    tokens = tok_all.at[0]
    for number, (name, src, dst) in enumerate(
        [("gate0", gate_in.at[0], gate.at[0]), ("up0", up_in.at[0], up.at[0])]
        + [("tokens", tokens_in, tokens)]
        + [(name + str(e), src.at[e], dst.at[e]) for e in range(1, local) for name, src, dst in
           (("gate", gate_in, gate), ("up", up_in, up))]
        + [("routes", routes_in, routes), ("scores", scores_in, scores), ("live", live_in, live)]
        + [("down", down_in, down)]
    ):
        loads[name] = pltpu.make_async_copy(src, dst, load.at[number])
        loads[name].start()

    mine = pl.multiple_of(me * rows, rows)

    def round_gate_up(e):
        loads["gate" + str(e)].wait()
        loads["up" + str(e)].wait()
        w_gu[e, pl.ds(mine, rows), :ff] = gate[e].astype(BF16)
        w_gu[e, pl.ds(mine, rows), ff:] = up[e].astype(BF16)

    round_gate_up(0)
    pl.semaphore_wait(barrier, len(partners))

    started = []

    def start(src, dst, send, recv, target, when=None):
        copy = pltpu.make_async_remote_copy(
            src_ref=src, dst_ref=dst, send_sem=send, recv_sem=recv,
            device_id=target, device_id_type=MESH,
        )
        started.append((copy, when))
        if when is None:
            copy.start()
        else:
            pl.when(when)(copy.start)

    halves = 2 if square else 1
    half_rows = rows // halves

    def piece(kind, key, owner):
        base = pl.multiple_of(owner * rows + key[-1] * half_rows, half_rows)
        if kind == "gu":
            return w_gu.at[key[0], pl.ds(base, half_rows), :]
        return w_down.at[pl.ds(base, half_rows), :]

    def sems(kind, key):
        if kind == "gu":
            index = key[0] * halves + key[1]
            return gu_send, gu_recv, index
        return down_send, down_recv, key[0]

    def send_piece(kind, key, owner, slot, target):
        send, recv, index = sems(kind, key)
        ref = piece(kind, key, owner)
        start(ref, ref, send.at[index, slot], recv.at[index, slot], device(target, holder))

    def wait_piece(kind, key, owner, slot):
        send, recv, index = sems(kind, key)
        ref = piece(kind, key, owner)
        pltpu.make_async_remote_copy(
            src_ref=ref, dst_ref=ref, send_sem=send.at[index, slot], recv_sem=recv.at[index, slot],
            device_id=device(sibling, holder), device_id_type=MESH,
        ).wait_recv()

    def turns(keys):
        if not square:
            return [(key, j) for key in keys for j in near]
        return [(keys[0], 1), (keys[1], 2), (keys[1], 1), (keys[0], 2)]

    def send_own(kind, some):
        for key, j in some:
            send_piece(kind, key, me, j, xor(me, 2 * j))

    def send_core(kind, keys):
        for key in keys:
            send_piece(kind, key, me, chips, sibling)

    def service_near(kind, some):
        for key, j in some:
            owner = xor(me, 2 * j)
            wait_piece(kind, key, owner, j)
            if square and (j == 1) == (key[-1] == 0):
                send_piece(kind, key, owner, 3, xor(me, 2 * (3 - j)))
            send_piece(kind, key, owner, chips + j, sibling)

    def service_far(kind, keys):
        if square:
            for key in keys:
                owner = xor(me, 6)
                wait_piece(kind, key, owner, 3)
                send_piece(kind, key, owner, chips + 3, sibling)

    def wait_sibling(kind, keys, j):
        for key in keys:
            wait_piece(kind, key, xor(sibling, 2 * j), chips + j)

    gu_keys = [[(e, a) for a in range(halves)] for e in range(local)]
    down_keys = [(a,) for a in range(halves)]

    def half_block(i, half):
        return tok_all.at[i, pl.ds(half * (block // 2), block // 2), :]

    def send_tokens(i):
        d, when = order[i], None
        if line and d != 2:
            when = jnp.logical_not(at_high if d == 1 else at_low)
        start(tokens, tok_all.at[i], tok_send.at[i], tok_recv.at[i], device(me, peer(d)), when)

    first_turns = turns(gu_keys[0])
    send_own("gu", first_turns[:2])
    loads["tokens"].wait()
    if line:
        for half in range(2):
            start(
                half_block(0, half), half_block(1, half), hand_send.at[half], hand_recv.at[half],
                device(me, peer(2)),
            )
    send_own("gu", first_turns[2:])
    for i in range(2 if line else 1, n_hold):
        send_tokens(i)
    for e in range(1, local):
        round_gate_up(e)
        send_own("gu", turns(gu_keys[e]))
    for e in range(local):
        send_core("gu", gu_keys[e])

    for name in ("routes", "scores", "live"):
        loads[name].wait()
    named_expert = routes[...].astype(F32)
    chosen = scores[...]
    chosen = chosen / jnp.sum(chosen, axis=0, keepdims=True)
    expert_id = lax.broadcasted_iota(jnp.int32, (experts, block), 0).astype(F32)
    weight = jnp.zeros((experts, block), F32)
    named = jnp.zeros((experts, block), F32)
    for k in range(top):
        hit = named_expert[k:k + 1] == expert_id
        weight = weight + jnp.where(hit, chosen[k:k + 1], 0.0)
        named = named + jnp.where(hit, 1.0, 0.0)
    alive = (live[...] > 0).astype(F32)
    named = named * alive
    before = (
        lax.broadcasted_iota(jnp.int32, (block, block), 0)
        < lax.broadcasted_iota(jnp.int32, (block, block), 1)
    ).astype(BF16)
    earlier = jnp.dot(named.astype(BF16), before, preferred_element_type=F32)
    weight = jnp.where((earlier < capacity) & (alive > 0), weight, 0.0)
    share_out[...] = jnp.zeros_like(share_out)
    for p in range(n_hold):
        share_out[p, :local, :] = weight[p * local:(p + 1) * local]
    for i in range(1, n_hold):
        start(
            share_out.at[peer(order[i])], share_in.at[i], share_send.at[i], share_recv.at[i],
            device(me, peer(order[i])),
        )

    loads["down"].wait()
    for e in range(local):
        w_down[pl.ds(mine, rows), e * ff:(e + 1) * ff] = down[e].astype(BF16)
    share_in[0] = share_out[holder]
    flip[...] = jnp.zeros_like(flip)
    if line:
        @pl.when(at_high)
        def _():
            back[order.index(1)] = jnp.zeros(back.shape[1:], BF16)

        @pl.when(at_low)
        def _():
            back[order.index(3)] = jnp.zeros(back.shape[1:], BF16)

    def arrive(dst, recv):
        pltpu.make_async_remote_copy(
            src_ref=dst, dst_ref=dst, send_sem=recv, recv_sem=recv,
            device_id=device(sibling, holder), device_id_type=MESH,
        ).wait_recv()

    far_slot = jnp.where(holder == 2, 3, 2)
    far_end = jnp.where(holder == 2, 3, 0)

    def hand_on(half):
        if line:
            arrive(half_block(1, half), hand_recv.at[half])
            start(
                half_block(1, half), half_block(far_slot, half),
                hand_send.at[2 + half], hand_recv.at[2 + half], device(me, far_end), inner,
            )

    for e in range(local):
        some = turns(gu_keys[e])
        if e == 0:
            service_near("gu", some[:2])
            hand_on(0)
            service_near("gu", some[2:])
            hand_on(1)
        else:
            service_near("gu", some)
        if e < local - 1:
            service_far("gu", gu_keys[e])
    send_core("down", down_keys)

    tile = 256
    per_group = 2

    def wait_tokens(i):
        if line and i > 1:
            from_end = at_high if order[i] == 3 else at_low

            @pl.when(from_end)
            def _():
                for half in range(2):
                    arrive(half_block(i, half), hand_recv.at[2 + half])

            pl.when(jnp.logical_not(from_end))(lambda: arrive(tok_all.at[i], tok_recv.at[i]))
        elif not line:
            arrive(tok_all.at[i], tok_recv.at[i])
        arrive(share_in.at[i], share_recv.at[i])

    def chip_product(first, e, j, at):
        base = pl.multiple_of(xor(chip, j) * 2 * rows, 2 * rows)
        return jnp.dot(
            tok_all[first:first + per_group, :, pl.ds(base, 2 * rows)].reshape(
                per_group * block, 2 * rows
            ),
            w_gu[e, pl.ds(base, 2 * rows), pl.ds(at, tile)], preferred_element_type=F32,
        )

    def early_group(first, e):
        def body(n, carry):
            at = pl.multiple_of(n * tile, tile)
            early[:, pl.ds(at, tile)] = (
                chip_product(first, e, 0, at) + chip_product(first, e, 1, at)
                + chip_product(first, e, 2, at)
            )
            return carry

        lax.fori_loop(0, 2 * ff // tile, body, 0)

    def hidden_group(first, e, resume=False):
        count = per_group * block
        flip[: per_group * 8] = share_in[first:first + per_group].reshape(per_group * 8, block)
        columns = flip[...].T
        picked = tok_all[first:first + per_group].reshape(count, width)
        scale = jnp.concatenate(
            [columns[:, i * 8 + e:i * 8 + e + 1] for i in range(per_group)], axis=0
        )

        def body(j, carry):
            at = pl.multiple_of(j * tile, tile)
            up_at = pl.multiple_of(ff + at, tile)
            if resume:
                g = early[:, pl.ds(at, tile)] + chip_product(first, e, 3, at)
                u = early[:, pl.ds(up_at, tile)] + chip_product(first, e, 3, up_at)
            else:
                g = jnp.dot(picked, w_gu[e, :, pl.ds(at, tile)], preferred_element_type=F32)
                u = jnp.dot(picked, w_gu[e, :, pl.ds(up_at, tile)], preferred_element_type=F32)
            value = (g / (1.0 + jnp.exp(-g))) * u * scale
            hidden[first * block:first * block + count,
                   pl.ds(pl.multiple_of(e * ff + at, tile), tile)] = value.astype(BF16)
            return carry

        lax.fori_loop(0, ff // tile, body, 0)

    parts, piece_width = back.shape[1], back.shape[3]

    def column(part):
        if parts == 1:
            return 0
        return pl.multiple_of(xor(chip, part) * piece_width, piece_width)

    def send_back(i, part, when=None):
        start(
            stage.at[i, part], back.at[i, part],
            ret_send.at[i, part], ret_recv.at[i, part],
            device(me, origin(order[i])), when,
        )

    def pass_on(part):
        @pl.when(inner)
        def _():
            arrive(relay.at[part], relay_recv.at[part])
            stage[1, part] = (ahead[part % 2] + relay[part].astype(F32)).astype(BF16)
        send_back(1, part, inner)

    def rows_out(part, first, count):
        at = column(part)
        value = lax.dot_general(
            hidden[first * block:(first + count) * block, :],
            w_down[pl.ds(at, piece_width), :], PAIR, preferred_element_type=F32,
        )
        stage[first:first + count, part] = value.astype(BF16).reshape(count, block, piece_width)
        if line and first == 0:
            ahead[part % 2] = value[block:2 * block]

    def send_relay(part):
        far = jnp.where(at_low, 2, 3)
        start(
            stage.at[far, part], relay.at[part], relay_send.at[part], relay_recv.at[part],
            device(me, jnp.where(at_low, 1, 2)), jnp.logical_not(inner),
        )

    def send_near(part):
        send_back(2, part, inner)
        send_back(3, part, inner)

    def send_near_end(part):
        send_back(2, part, at_high)
        send_back(3, part, at_low)

    if line:
        wait_tokens(1)
        for e in range(local):
            last = e == local - 1
            if last:
                service_far("gu", gu_keys[e])
                send_own("down", turns(down_keys))
            for j in range(chips):
                if not last:
                    wait_sibling("gu", gu_keys[e], j)
            if not last:
                hidden_group(0, e)
        for i in range(2, n_hold):
            wait_tokens(i)
        for e in range(local - 1):
            hidden_group(2, e)
        for j in range(chips):
            wait_sibling("gu", gu_keys[local - 1], j)
            if j == 2:
                early_group(2, local - 1)
        hidden_group(2, local - 1, True)
        wait_sibling("down", down_keys, 0)
        rows_out(0, 2, 2)
        send_relay(0)
        send_near(0)
        send_near_end(0)
        hidden_group(0, local - 1)
        rows_out(0, 0, 2)
        send_back(1, 0, jnp.logical_not(inner))
        down_turns = turns(down_keys)
        service_near("down", down_turns[:2])
        pass_on(0)
        service_near("down", down_turns[2:])
        for part in range(1, parts):
            if part == parts - 1:
                service_far("down", down_keys)
            wait_sibling("down", down_keys, part)
            rows_out(part, 0, n_hold)
            send_relay(part)
            send_back(1, part, jnp.logical_not(inner))
            send_near(part)
            if part > 1:
                send_near_end(part - 1)
            if part == parts - 1:
                send_near_end(part)
            if part > 1:
                pass_on(part - 1)
        pass_on(parts - 1)
    else:
        for e in range(local):
            if e == local - 1:
                service_far("gu", gu_keys[e])
                send_own("down", turns(down_keys))
            for j in range(chips):
                wait_sibling("gu", gu_keys[e], j)
        service_near("down", turns(down_keys))
        service_far("down", down_keys)
        for j in range(chips):
            wait_sibling("down", down_keys, j)
        for i in range(1, n_hold):
            wait_tokens(i)
        for first in range(0, n_hold, per_group):
            for e in range(local):
                hidden_group(first, e)
            for part in range(parts):
                rows_out(part, first, per_group)
                for i in range(first, first + per_group):
                    if i > 0:
                        send_back(i, part)

    for part in range(parts):
        total = stage[0, part].astype(F32)
        for i in range(1, n_hold):
            def landed(i=i, part=part):
                arrive(back.at[i, part], ret_recv.at[i, part])
            if line and i > 1:
                pl.when(jnp.logical_not(at_high if order[i] == 1 else at_low))(landed)
            else:
                landed()
            total = total + back[i, part].astype(F32)
        out[:, pl.ds(column(part), piece_width)] = total.astype(BF16)

    for copy, when in started:
        if when is None:
            copy.wait_send()
        else:
            pl.when(when)(copy.wait_send)


def local(n_group, n_hold, tokens, gate, up, down, routes, scores, live):
    experts_here, rows, ff = gate.shape
    block, width = tokens.shape
    down, routes, scores = jnp.swapaxes(down, 1, 2), routes.T, scores.T
    top = routes.shape[0]
    capacity = block * top // (experts_here * n_hold)
    chips = n_group // 2
    halves = 2 if chips == 4 else 1
    parts = chips if (2 * rows) % 128 == 0 else 1
    dma = pltpu.SemaphoreType.DMA
    vmem = pl.BlockSpec(memory_space=pltpu.VMEM)
    return pl.pallas_call(
        functools.partial(kernel, n_group, n_hold, capacity),
        out_shape=pltpu.VMEM((block, width), BF16),
        in_specs=[pl.BlockSpec(memory_space=pltpu.HBM)] * 7,
        out_specs=vmem,
        scratch_shapes=[
            pltpu.VMEM(gate.shape, F32),
            pltpu.VMEM(up.shape, F32),
            pltpu.VMEM(down.shape, F32),
            pltpu.VMEM(routes.shape, jnp.int32),
            pltpu.VMEM(scores.shape, F32),
            pltpu.VMEM((1, block), jnp.int32),
            dma((5 + 2 * experts_here,)),
            pltpu.VMEM((experts_here, width, 2 * ff), BF16),
            pltpu.VMEM((width, experts_here * ff), BF16),
            pltpu.VMEM((n_hold, block, width), BF16),
            pltpu.VMEM((n_hold, 8, block), F32),
            pltpu.VMEM((n_hold, 8, block), F32),
            pltpu.VMEM((n_hold * block, experts_here * ff), BF16),
            pltpu.VMEM((n_hold, parts, block, width // parts), BF16),
            pltpu.VMEM((n_hold, parts, block, width // parts), BF16),
            pltpu.VMEM((128, 128), F32),
            pltpu.VMEM((parts, block, width // parts), BF16),
            pltpu.VMEM((2, block, width // parts), F32),
            pltpu.VMEM((2 * block, 2 * ff), F32),
            dma((experts_here * halves, 2 * chips)),
            dma((experts_here * halves, 2 * chips)),
            dma((halves, 2 * chips)),
            dma((halves, 2 * chips)),
            dma((n_hold,)),
            dma((n_hold,)),
            dma((n_hold,)),
            dma((n_hold,)),
            dma((n_hold, parts)),
            dma((n_hold, parts)),
            dma((parts,)),
            dma((parts,)),
            dma((4,)),
            dma((4,)),
        ],
        compiler_params=pltpu.CompilerParams(
            collective_id=0, has_side_effects=True, vmem_limit_bytes=58 * 2**20
        ),
    )(tokens, gate, up, down, routes, scores, live.reshape(1, block))


def solution(mesh):
    in_specs = (
        P(("group", "expert"), None),
        P("expert", "group", None),
        P("expert", "group", None),
        P("expert", None, "group"),
        P(("group", "expert"), None),
        P(("group", "expert"), None),
        P(("group", "expert")),
    )
    out_specs = P(("group", "expert"), None)
    body = functools.partial(local, mesh.shape["group"], mesh.shape["expert"])
    return jax.shard_map(body, mesh=mesh, in_specs=in_specs, out_specs=out_specs, check_vma=False)
```

```python
import functools

import jax
import jax.numpy as jnp
from jax import lax
from jax.experimental import pallas as pl
from jax.experimental.pallas import tpu as pltpu
from jax.sharding import PartitionSpec as P

MESH = pl.DeviceIdType.MESH
F32, BF16 = jnp.float32, jnp.bfloat16
PAIR = (((1,), (1,)), ((), ()))


def xor(value, mask):
    bit = 1
    while bit <= mask:
        if mask & bit:
            value = value + bit * (1 - 2 * ((value // bit) % 2))
        bit *= 2
    return value


def kernel(
    n_group, n_hold, capacity,
    tokens_in, gate_in, up_in, down_in, routes_in, scores_in, live_in, out,
    gate, up, down, routes, scores, live, load, w_gu, w_down, tok_all, share_out, share_in, hidden, stage, back, flip, relay, ahead, early,
    gu_send, gu_recv, down_send, down_recv, tok_send, tok_recv, share_send, share_recv,
    ret_send, ret_recv, relay_send, relay_recv, hand_send, hand_recv,
):
    local, rows, ff = gate.shape
    block, width = tokens_in.shape
    top = routes.shape[0]
    experts = local * n_hold
    chips = n_group // 2
    square = chips == 4
    me, holder = lax.axis_index("group"), lax.axis_index("expert")
    chip = me // 2
    sibling = xor(me, 1)

    def device(group, expert):
        return (group, expert)

    line = n_hold == 4 and square and rows % 64 == 0
    order = (0, 2, 1, 3) if line else tuple(range(n_hold))
    at_low, at_high = holder == 0, holder == n_hold - 1
    inner = jnp.logical_not(jnp.logical_or(at_low, at_high))

    def peer(d):
        return lax.rem(holder + d, n_hold)

    def origin(d):
        return lax.rem(holder + n_hold - d, n_hold)

    near = (1, 2) if square else tuple(range(1, chips))
    barrier = pltpu.get_barrier_semaphore()
    partners = [device(xor(me, 2 * j), holder) for j in near] + [device(sibling, holder)]
    partners += [device(me, peer(d)) for d in range(1, n_hold)]
    for partner in partners:
        pl.semaphore_signal(barrier, inc=1, device_id=partner, device_id_type=MESH)
    loads = {}
    tokens = tok_all.at[0]
    for number, (name, src, dst) in enumerate(
        [("gate0", gate_in.at[0], gate.at[0]), ("up0", up_in.at[0], up.at[0])]
        + [("tokens", tokens_in, tokens)]
        + [(name + str(e), src.at[e], dst.at[e]) for e in range(1, local) for name, src, dst in
           (("gate", gate_in, gate), ("up", up_in, up))]
        + [("routes", routes_in, routes), ("scores", scores_in, scores), ("live", live_in, live)]
        + [("down", down_in, down)]
    ):
        loads[name] = pltpu.make_async_copy(src, dst, load.at[number])
        loads[name].start()

    mine = pl.multiple_of(me * rows, rows)

    def round_gate_up(e):
        loads["gate" + str(e)].wait()
        loads["up" + str(e)].wait()
        w_gu[e, pl.ds(mine, rows), :ff] = gate[e].astype(BF16)
        w_gu[e, pl.ds(mine, rows), ff:] = up[e].astype(BF16)

    round_gate_up(0)
    pl.semaphore_wait(barrier, len(partners))

    started = []

    def start(src, dst, send, recv, target, when=None):
        copy = pltpu.make_async_remote_copy(
            src_ref=src, dst_ref=dst, send_sem=send, recv_sem=recv,
            device_id=target, device_id_type=MESH,
        )
        started.append((copy, when))
        if when is None:
            copy.start()
        else:
            pl.when(when)(copy.start)

    halves = 2 if square else 1
    half_rows = rows // halves

    def piece(kind, key, owner):
        base = pl.multiple_of(owner * rows + key[-1] * half_rows, half_rows)
        if kind == "gu":
            return w_gu.at[key[0], pl.ds(base, half_rows), :]
        return w_down.at[pl.ds(base, half_rows), :]

    def sems(kind, key):
        if kind == "gu":
            index = key[0] * halves + key[1]
            return gu_send, gu_recv, index
        return down_send, down_recv, key[0]

    def send_piece(kind, key, owner, slot, target):
        send, recv, index = sems(kind, key)
        ref = piece(kind, key, owner)
        start(ref, ref, send.at[index, slot], recv.at[index, slot], device(target, holder))

    def wait_piece(kind, key, owner, slot):
        send, recv, index = sems(kind, key)
        ref = piece(kind, key, owner)
        pltpu.make_async_remote_copy(
            src_ref=ref, dst_ref=ref, send_sem=send.at[index, slot], recv_sem=recv.at[index, slot],
            device_id=device(sibling, holder), device_id_type=MESH,
        ).wait_recv()

    def turns(keys):
        if not square:
            return [(key, j) for key in keys for j in near]
        return [(keys[0], 1), (keys[1], 2), (keys[1], 1), (keys[0], 2)]

    def send_own(kind, some):
        for key, j in some:
            send_piece(kind, key, me, j, xor(me, 2 * j))

    def send_core(kind, keys):
        for key in keys:
            send_piece(kind, key, me, chips, sibling)

    def service_near(kind, some):
        for key, j in some:
            owner = xor(me, 2 * j)
            wait_piece(kind, key, owner, j)
            if square and (j == 1) == (key[-1] == 0):
                send_piece(kind, key, owner, 3, xor(me, 2 * (3 - j)))
            send_piece(kind, key, owner, chips + j, sibling)

    def service_far(kind, keys):
        if square:
            for key in keys:
                owner = xor(me, 6)
                wait_piece(kind, key, owner, 3)
                send_piece(kind, key, owner, chips + 3, sibling)

    def wait_sibling(kind, keys, j):
        for key in keys:
            wait_piece(kind, key, xor(sibling, 2 * j), chips + j)

    gu_keys = [[(e, a) for a in range(halves)] for e in range(local)]
    down_keys = [(a,) for a in range(halves)]

    def half_block(i, half):
        return tok_all.at[i, pl.ds(half * (block // 2), block // 2), :]

    def send_tokens(i):
        d, when = order[i], None
        if line and d != 2:
            when = jnp.logical_not(at_high if d == 1 else at_low)
        start(tokens, tok_all.at[i], tok_send.at[i], tok_recv.at[i], device(me, peer(d)), when)

    first_turns = turns(gu_keys[0])
    send_own("gu", first_turns[:2])
    loads["tokens"].wait()
    if line:
        for half in range(2):
            start(
                half_block(0, half), half_block(1, half), hand_send.at[half], hand_recv.at[half],
                device(me, peer(2)),
            )
    send_own("gu", first_turns[2:])
    for i in range(2 if line else 1, n_hold):
        send_tokens(i)
    for e in range(1, local):
        round_gate_up(e)
        send_own("gu", turns(gu_keys[e]))
    for e in range(local):
        send_core("gu", gu_keys[e])

    for name in ("routes", "scores", "live"):
        loads[name].wait()
    named_expert = routes[...].astype(F32)
    chosen = scores[...]
    chosen = chosen / jnp.sum(chosen, axis=0, keepdims=True)
    expert_id = lax.broadcasted_iota(jnp.int32, (experts, block), 0).astype(F32)
    weight = jnp.zeros((experts, block), F32)
    named = jnp.zeros((experts, block), F32)
    for k in range(top):
        hit = named_expert[k:k + 1] == expert_id
        weight = weight + jnp.where(hit, chosen[k:k + 1], 0.0)
        named = named + jnp.where(hit, 1.0, 0.0)
    alive = (live[...] > 0).astype(F32)
    named = named * alive
    before = (
        lax.broadcasted_iota(jnp.int32, (block, block), 0)
        < lax.broadcasted_iota(jnp.int32, (block, block), 1)
    ).astype(BF16)
    earlier = jnp.dot(named.astype(BF16), before, preferred_element_type=F32)
    weight = jnp.where((earlier < capacity) & (alive > 0), weight, 0.0)
    share_out[...] = jnp.zeros_like(share_out)
    for p in range(n_hold):
        share_out[p, :local, :] = weight[p * local:(p + 1) * local]
    for i in range(1, n_hold):
        start(
            share_out.at[peer(order[i])], share_in.at[i], share_send.at[i], share_recv.at[i],
            device(me, peer(order[i])),
        )

    loads["down"].wait()
    for e in range(local):
        w_down[pl.ds(mine, rows), e * ff:(e + 1) * ff] = down[e].astype(BF16)
    share_in[0] = share_out[holder]
    flip[...] = jnp.zeros_like(flip)
    if line:
        @pl.when(at_high)
        def _():
            back[order.index(1)] = jnp.zeros(back.shape[1:], BF16)

        @pl.when(at_low)
        def _():
            back[order.index(3)] = jnp.zeros(back.shape[1:], BF16)

    def arrive(dst, recv):
        pltpu.make_async_remote_copy(
            src_ref=dst, dst_ref=dst, send_sem=recv, recv_sem=recv,
            device_id=device(sibling, holder), device_id_type=MESH,
        ).wait_recv()

    far_slot = jnp.where(holder == 2, 3, 2)
    far_end = jnp.where(holder == 2, 3, 0)

    def hand_on(half):
        if line:
            arrive(half_block(1, half), hand_recv.at[half])
            start(
                half_block(1, half), half_block(far_slot, half),
                hand_send.at[2 + half], hand_recv.at[2 + half], device(me, far_end), inner,
            )

    for e in range(local):
        some = turns(gu_keys[e])
        if e == 0:
            service_near("gu", some[:2])
            hand_on(0)
            service_near("gu", some[2:])
            hand_on(1)
        else:
            service_near("gu", some)
        if e < local - 1:
            service_far("gu", gu_keys[e])
    send_core("down", down_keys)

    tile = 256
    per_group = 2

    def wait_tokens(i):
        if line and i > 1:
            from_end = at_high if order[i] == 3 else at_low

            @pl.when(from_end)
            def _():
                for half in range(2):
                    arrive(half_block(i, half), hand_recv.at[2 + half])

            pl.when(jnp.logical_not(from_end))(lambda: arrive(tok_all.at[i], tok_recv.at[i]))
        elif not line:
            arrive(tok_all.at[i], tok_recv.at[i])
        arrive(share_in.at[i], share_recv.at[i])

    def chip_product(first, e, j, at):
        base = pl.multiple_of(xor(chip, j) * 2 * rows, 2 * rows)
        return jnp.dot(
            tok_all[first:first + per_group, :, pl.ds(base, 2 * rows)].reshape(
                per_group * block, 2 * rows
            ),
            w_gu[e, pl.ds(base, 2 * rows), pl.ds(at, tile)], preferred_element_type=F32,
        )

    def early_group(first, e):
        def body(n, carry):
            at = pl.multiple_of(n * tile, tile)
            early[:, pl.ds(at, tile)] = (
                chip_product(first, e, 0, at) + chip_product(first, e, 1, at)
                + chip_product(first, e, 2, at)
            )
            return carry

        lax.fori_loop(0, 2 * ff // tile, body, 0)

    def hidden_group(first, e, resume=False):
        count = per_group * block
        flip[: per_group * 8] = share_in[first:first + per_group].reshape(per_group * 8, block)
        columns = flip[...].T
        picked = tok_all[first:first + per_group].reshape(count, width)
        scale = jnp.concatenate(
            [columns[:, i * 8 + e:i * 8 + e + 1] for i in range(per_group)], axis=0
        )

        def body(j, carry):
            at = pl.multiple_of(j * tile, tile)
            up_at = pl.multiple_of(ff + at, tile)
            if resume:
                g = early[:, pl.ds(at, tile)] + chip_product(first, e, 3, at)
                u = early[:, pl.ds(up_at, tile)] + chip_product(first, e, 3, up_at)
            else:
                g = jnp.dot(picked, w_gu[e, :, pl.ds(at, tile)], preferred_element_type=F32)
                u = jnp.dot(picked, w_gu[e, :, pl.ds(up_at, tile)], preferred_element_type=F32)
            value = (g / (1.0 + jnp.exp(-g))) * u * scale
            hidden[first * block:first * block + count,
                   pl.ds(pl.multiple_of(e * ff + at, tile), tile)] = value.astype(BF16)
            return carry

        lax.fori_loop(0, ff // tile, body, 0)

    parts, piece_width = back.shape[1], back.shape[3]

    def column(part):
        if parts == 1:
            return 0
        return pl.multiple_of(xor(chip, part) * piece_width, piece_width)

    def send_back(i, part, when=None):
        start(
            stage.at[i, part], back.at[i, part],
            ret_send.at[i, part], ret_recv.at[i, part],
            device(me, origin(order[i])), when,
        )

    def pass_on(part):
        @pl.when(inner)
        def _():
            arrive(relay.at[part], relay_recv.at[part])
            stage[1, part] = (ahead[part % 2] + relay[part].astype(F32)).astype(BF16)
        send_back(1, part, inner)

    def rows_out(part, first, count):
        at = column(part)
        value = lax.dot_general(
            hidden[first * block:(first + count) * block, :],
            w_down[pl.ds(at, piece_width), :], PAIR, preferred_element_type=F32,
        )
        stage[first:first + count, part] = value.astype(BF16).reshape(count, block, piece_width)
        if line and first == 0:
            ahead[part % 2] = value[block:2 * block]

    def send_relay(part):
        far = jnp.where(at_low, 2, 3)
        start(
            stage.at[far, part], relay.at[part], relay_send.at[part], relay_recv.at[part],
            device(me, jnp.where(at_low, 1, 2)), jnp.logical_not(inner),
        )

    def send_near(part):
        send_back(2, part, inner)
        send_back(3, part, inner)

    def send_near_end(part):
        send_back(2, part, at_high)
        send_back(3, part, at_low)

    if line:
        wait_tokens(1)
        for e in range(local):
            last = e == local - 1
            if last:
                send_own("down", turns(down_keys)[:2])
                service_far("gu", gu_keys[e])
                send_own("down", turns(down_keys)[2:])
            for j in range(chips):
                if not last:
                    wait_sibling("gu", gu_keys[e], j)
            if not last:
                hidden_group(0, e)
        for i in range(2, n_hold):
            wait_tokens(i)
        for e in range(local - 1):
            hidden_group(2, e)
        for j in range(chips):
            wait_sibling("gu", gu_keys[local - 1], j)
            if j == 2:
                early_group(2, local - 1)
        hidden_group(2, local - 1, True)
        wait_sibling("down", down_keys, 0)
        rows_out(0, 2, 2)
        send_relay(0)
        send_near(0)
        send_near_end(0)
        hidden_group(0, local - 1)
        rows_out(0, 0, 2)
        send_back(1, 0, jnp.logical_not(inner))
        down_turns = turns(down_keys)
        service_near("down", down_turns[:2])
        pass_on(0)
        service_near("down", down_turns[2:])
        for part in range(1, parts):
            if part == parts - 1:
                service_far("down", down_keys)
            wait_sibling("down", down_keys, part)
            rows_out(part, 0, n_hold)
            send_relay(part)
            send_back(1, part, jnp.logical_not(inner))
            send_near(part)
            if part > 1:
                send_near_end(part - 1)
            if part == parts - 1:
                send_near_end(part)
            if part > 1:
                pass_on(part - 1)
        pass_on(parts - 1)
    else:
        for e in range(local):
            if e == local - 1:
                service_far("gu", gu_keys[e])
                send_own("down", turns(down_keys))
            for j in range(chips):
                wait_sibling("gu", gu_keys[e], j)
        service_near("down", turns(down_keys))
        service_far("down", down_keys)
        for j in range(chips):
            wait_sibling("down", down_keys, j)
        for i in range(1, n_hold):
            wait_tokens(i)
        for first in range(0, n_hold, per_group):
            for e in range(local):
                hidden_group(first, e)
            for part in range(parts):
                rows_out(part, first, per_group)
                for i in range(first, first + per_group):
                    if i > 0:
                        send_back(i, part)

    for part in range(parts):
        total = stage[0, part].astype(F32)
        for i in range(1, n_hold):
            def landed(i=i, part=part):
                arrive(back.at[i, part], ret_recv.at[i, part])
            if line and i > 1:
                pl.when(jnp.logical_not(at_high if order[i] == 1 else at_low))(landed)
            else:
                landed()
            total = total + back[i, part].astype(F32)
        out[:, pl.ds(column(part), piece_width)] = total.astype(BF16)

    for copy, when in started:
        if when is None:
            copy.wait_send()
        else:
            pl.when(when)(copy.wait_send)


def local(n_group, n_hold, tokens, gate, up, down, routes, scores, live):
    experts_here, rows, ff = gate.shape
    block, width = tokens.shape
    down, routes, scores = jnp.swapaxes(down, 1, 2), routes.T, scores.T
    top = routes.shape[0]
    capacity = block * top // (experts_here * n_hold)
    chips = n_group // 2
    halves = 2 if chips == 4 else 1
    parts = chips if (2 * rows) % 128 == 0 else 1
    dma = pltpu.SemaphoreType.DMA
    vmem = pl.BlockSpec(memory_space=pltpu.VMEM)
    return pl.pallas_call(
        functools.partial(kernel, n_group, n_hold, capacity),
        out_shape=pltpu.VMEM((block, width), BF16),
        in_specs=[pl.BlockSpec(memory_space=pltpu.HBM)] * 7,
        out_specs=vmem,
        scratch_shapes=[
            pltpu.VMEM(gate.shape, F32),
            pltpu.VMEM(up.shape, F32),
            pltpu.VMEM(down.shape, F32),
            pltpu.VMEM(routes.shape, jnp.int32),
            pltpu.VMEM(scores.shape, F32),
            pltpu.VMEM((1, block), jnp.int32),
            dma((5 + 2 * experts_here,)),
            pltpu.VMEM((experts_here, width, 2 * ff), BF16),
            pltpu.VMEM((width, experts_here * ff), BF16),
            pltpu.VMEM((n_hold, block, width), BF16),
            pltpu.VMEM((n_hold, 8, block), F32),
            pltpu.VMEM((n_hold, 8, block), F32),
            pltpu.VMEM((n_hold * block, experts_here * ff), BF16),
            pltpu.VMEM((n_hold, parts, block, width // parts), BF16),
            pltpu.VMEM((n_hold, parts, block, width // parts), BF16),
            pltpu.VMEM((128, 128), F32),
            pltpu.VMEM((parts, block, width // parts), BF16),
            pltpu.VMEM((2, block, width // parts), F32),
            pltpu.VMEM((2 * block, 2 * ff), F32),
            dma((experts_here * halves, 2 * chips)),
            dma((experts_here * halves, 2 * chips)),
            dma((halves, 2 * chips)),
            dma((halves, 2 * chips)),
            dma((n_hold,)),
            dma((n_hold,)),
            dma((n_hold,)),
            dma((n_hold,)),
            dma((n_hold, parts)),
            dma((n_hold, parts)),
            dma((parts,)),
            dma((parts,)),
            dma((4,)),
            dma((4,)),
        ],
        compiler_params=pltpu.CompilerParams(
            collective_id=0, has_side_effects=True, vmem_limit_bytes=58 * 2**20
        ),
    )(tokens, gate, up, down, routes, scores, live.reshape(1, block))


def solution(mesh):
    in_specs = (
        P(("group", "expert"), None),
        P("expert", "group", None),
        P("expert", "group", None),
        P("expert", None, "group"),
        P(("group", "expert"), None),
        P(("group", "expert"), None),
        P(("group", "expert")),
    )
    out_specs = P(("group", "expert"), None)
    body = functools.partial(local, mesh.shape["group"], mesh.shape["expert"])
    return jax.shard_map(body, mesh=mesh, in_specs=in_specs, out_specs=out_specs, check_vma=False)
```
